32 devices in a mesh: dp: 2 (over x), pipe: 2 (over core), ctx: 8 (over z, y).
Axes of the slice: x: 2, y: 2, z: 4, core: 2. Of those that a mesh axis runs over, the one named last changes fastest.
Arguments:
- section_input: bfloat16 [2, 2, 1024, 2048], P('dp', 'pipe', 'ctx'), may hold values from -6 to 6
- section_positions: int32 [2, 2, 1024], P('dp', 'pipe', 'ctx'), may hold values from 0 to 1023, as said below
- saved_input: bfloat16 [2, 2, 1024, 2048], P('dp', 'pipe', 'ctx'), may hold values from -6 to 6
- saved_positions: int32 [2, 2, 1024], P('dp', 'pipe', 'ctx'), may hold values from 0 to 1023, as said below
- cotangent: bfloat16 [2, 2, 1024, 2048], P('dp', 'pipe', 'ctx'), may hold values from -6 to 6
- norm_gains: float32 [2, 2, 2, 2048], P(None, 'pipe'), may hold values from -2 to 2
- output_gains: float32 [2, 2, 2048], P(None, 'pipe'), may hold values from 0.25 to 2
- plan: int32 [2, 2, 2], P('dp', 'pipe'), may hold values from 0 to 1
Outputs:
- next_input: bfloat16 [2, 2, 1024, 2048], P('dp', 'pipe', 'ctx')
- upstream_grad: bfloat16 [2, 2, 1024, 2048], P('dp', 'pipe', 'ctx')
- gain_grads: float32 [2, 3, 2048], P('pipe')
The draws below stay inside these ranges and needn't reach their ends.
Inputs may be any that keep to these rules, and one draw needn't show every extreme that they name: `section_positions`: in every sequence the first position is 0 and each later one is either one more than the position before it or 0 (a new document). `saved_positions`: in every sequence the first position is 0 and each later one is either one more than the position before it or 0 (a new document).
All inputs are finite; a program needn't handle non-finite values.
Results may differ from the reference program's by a relative error of at most 0.0075.
Values may be sent and summed in bfloat16 or wider, within the bound.
A program may use at most 64 MiB of HBM per device.

```python
import math
import jax
import jax.numpy as jnp
from jax import lax

HEADS = 16
HEAD_DIM = 128
FEATURES = 2048
WINDOW = 512
TOK_DEV = 128
SEQ_LEN = 1024
N_DP = 2
N_PIPE = 2
N_CTX = 8


def document_positions(key, salt):
    period = min(4 * WINDOW, SEQ_LEN)
    random_starts = jax.random.randint(jax.random.fold_in(key, salt), (N_DP, N_PIPE, SEQ_LEN), 0, 2 * WINDOW) == 0
    offsets = lax.broadcasted_iota(jnp.int32, (N_DP, N_PIPE, SEQ_LEN), 2)
    replica_ids = lax.broadcasted_iota(jnp.int32, (N_DP, N_PIPE, SEQ_LEN), 0)
    section_ids = lax.broadcasted_iota(jnp.int32, (N_DP, N_PIPE, SEQ_LEN), 1)
    kept_whole = (replica_ids == 0) & (section_ids == 0) & (offsets < period)
    starts = random_starts & jnp.logical_not(kept_whole) | (offsets % period == 0)
    latest = lax.cummax(jnp.where(starts, offsets, 0), axis=2)
    return (offsets - latest).astype(jnp.int32)


def draw_section_positions(key, part):
    return document_positions(key, 11)


def draw_saved_positions(key, part):
    return document_positions(key, 23)


def with_ends(drawn, rng, low, high):
    longest = drawn.shape.index(max(drawn.shape))
    spots = []
    for shift in (0, 1):
        where = [jax.random.randint(jax.random.fold_in(rng, axis), (), 0, length) for axis, length in enumerate(drawn.shape)]
        where[longest] = (where[longest] + shift) % drawn.shape[longest]
        spots.append(tuple(where))
    return drawn.at[spots[0]].set(low).at[spots[1]].set(high)


def shard_levels(own_key, dims, pieces, smallest, largest):
    factor_of = 1.0
    for dim, shards_of in pieces:
        steps = jax.random.uniform(jax.random.fold_in(jax.random.fold_in(own_key, 6), dim), (shards_of,), jnp.float32, smallest / len(pieces), largest / len(pieces))
        factor_of = factor_of * jnp.repeat(jnp.exp(steps), dims[dim] // shards_of).reshape((-1,) + (1,) * (len(dims) - 1 - dim))
    return factor_of


def noise(own_key, dims, scale, reach, cuts=(), kind=jnp.bfloat16):
    drawn = jax.random.normal(own_key, dims, jnp.float32) * scale
    if len(cuts) > 0:
        drawn = shard_levels(own_key, dims, cuts, -0.22, 0.18) * drawn
    return jnp.clip(drawn, min=-reach, max=reach).astype(kind)


def setup_inputs(seed: int = 0) -> dict:
    keys = jax.random.split(jax.random.key(seed), 9)
    section_input = noise(keys[0], (N_DP, N_PIPE, SEQ_LEN, FEATURES), 1.0, 6.0, ((0, 2), (1, 2), (2, 8)))
    section_positions = draw_section_positions(jax.random.fold_in(keys[8], 71), 0)
    saved_input = noise(keys[2], (N_DP, N_PIPE, SEQ_LEN, FEATURES), 1.0, 6.0, ((0, 2), (1, 2), (2, 8)))
    saved_positions = draw_saved_positions(jax.random.fold_in(keys[8], 71), 0)
    cotangent = noise(keys[4], (N_DP, N_PIPE, SEQ_LEN, FEATURES), 1.0, 6.0, ((0, 2), (1, 2), (2, 8)))
    norm_gains = jnp.clip(jax.random.uniform(keys[5], (2, N_PIPE, 2, FEATURES), jnp.float32, -2.0, 2.0) * shard_levels(keys[5], (2, N_PIPE, 2, FEATURES), ((1, 2),), -0.4, 0.0), -2.0, 2.0)
    output_gains = jnp.clip(jnp.exp(math.log(2.0) - 2.0794415 * jax.random.uniform(keys[6], (2, N_PIPE, FEATURES), jnp.float32) ** shard_levels(keys[6], (2, N_PIPE, FEATURES), ((1, 2),), -0.2, 0.2)), 0.25, 2.0)
    plan = with_ends(jax.random.randint(keys[7], (N_DP, N_PIPE, 2), 0, 2), jax.random.fold_in(keys[7], 1), 0, 1).astype(jnp.int32)
    return dict(section_input=section_input, section_positions=section_positions, saved_input=saved_input, saved_positions=saved_positions, cotangent=cotangent, norm_gains=norm_gains, output_gains=output_gains, plan=plan)


EPSILON = 1e-06

def as_bfloat(values):
    narrow = lax.optimization_barrier(values.astype(jnp.bfloat16)).astype(jnp.float32)
    return values + lax.stop_gradient(narrow - values)

def attend(key_rows, key_pos, key_ok, gains, query_count):
    total_rows = key_rows.shape[0]
    first_row = total_rows - query_count
    shaped = key_rows.reshape(total_rows, HEADS, HEAD_DIM)
    normed = shaped * lax.rsqrt(lax.optimization_barrier(jnp.mean(shaped * shaped, axis=-1, keepdims=True)) + EPSILON)
    query_gain = gains[0].reshape(HEADS, HEAD_DIM)
    key_gain = gains[1].reshape(HEADS, HEAD_DIM)
    queries = as_bfloat(normed[first_row:] * query_gain)
    key_vecs = as_bfloat(normed * key_gain)
    scores = jnp.einsum('qhe,khe->hqk', queries, key_vecs) / jnp.sqrt(jnp.float32(HEAD_DIM))
    query_ids = first_row + jnp.arange(query_count, dtype=jnp.int32)
    key_ids = jnp.arange(total_rows, dtype=jnp.int32)
    distance = query_ids[:, None] - key_ids[None, :]
    query_pos = key_pos[first_row:]
    allowed = (distance >= 0) & (distance < WINDOW) & (query_pos[:, None] - key_pos[None, :] == distance) & key_ok[None, :]
    weights = jnp.where(allowed[None], jnp.exp(scores), jnp.float32(0.0))
    probability = as_bfloat(weights / lax.optimization_barrier(jnp.sum(weights, axis=-1, keepdims=True)))
    mixture = jnp.einsum('hqk,khe->qhe', probability, shaped)
    return key_rows[first_row:] + mixture.reshape(query_count, FEATURES) * gains[2]

def padded_sequence(rows32, positions):
    padded = jnp.concatenate([jnp.zeros((WINDOW, FEATURES), jnp.float32), rows32], axis=0)
    pos_pad = jnp.concatenate([jnp.zeros((WINDOW,), jnp.int32), positions.astype(jnp.int32)], axis=0)
    valid = jnp.concatenate([jnp.zeros((WINDOW,), bool), jnp.ones((SEQ_LEN,), bool)], axis=0)
    return (padded, pos_pad, valid)

def select_gains(norm_gains, output_gains, lap_index, section_index):
    pair_gains = norm_gains[lap_index, section_index]
    return jnp.concatenate([pair_gains, output_gains[lap_index, section_index][None]], axis=0)

def reference(section_input, section_positions, saved_input, saved_positions, cotangent, norm_gains, output_gains, plan):
    pair_count = N_DP * N_PIPE
    span = WINDOW + TOK_DEV
    piece_len = min(WINDOW, TOK_DEV)
    piece_count = WINDOW // piece_len

    def one_pair(operands):
        inputs, positions, saved_rows, saved_pos, cot_rows, pair_index = operands
        section_index = pair_index % N_PIPE
        replica_index = pair_index // N_PIPE
        forward_gains = select_gains(norm_gains, output_gains, plan[replica_index, section_index, 0], section_index)
        backward_gains = select_gains(norm_gains, output_gains, plan[replica_index, section_index, 1], section_index)
        padded, pos_pad, valid = padded_sequence(inputs.astype(jnp.float32), positions)
        outputs = []
        for shard in range(N_CTX):
            start = shard * TOK_DEV
            outputs.append(attend(padded[start:start + span], pos_pad[start:start + span], valid[start:start + span], forward_gains, TOK_DEV))
        produced = jnp.concatenate(outputs, axis=0).astype(jnp.bfloat16)
        s_pad, s_pos, s_valid = padded_sequence(saved_rows.astype(jnp.float32), saved_pos)
        grad_total = jnp.zeros((WINDOW + SEQ_LEN, FEATURES), jnp.float32)
        gain_total = jnp.zeros((3, FEATURES), jnp.float32)
        for shard in range(N_CTX):
            start = shard * TOK_DEV
            these_pos = s_pos[start:start + span]
            these_ok = s_valid[start:start + span]

            def local_layer(rows, gains):
                return attend(rows, these_pos, these_ok, gains, TOK_DEV)
            _, pullback = jax.vjp(local_layer, s_pad[start:start + span], backward_gains)
            key_grads, gain_grad = pullback(cot_rows[start:start + TOK_DEV].astype(jnp.float32))
            rim = lax.optimization_barrier(key_grads[:WINDOW].astype(jnp.bfloat16)).astype(jnp.float32)
            for piece in range(piece_count):
                lo = start + piece * piece_len
                grad_total = grad_total.at[lo:lo + piece_len].add(rim[piece * piece_len:(piece + 1) * piece_len])
            grad_total = grad_total.at[start + WINDOW:start + span].add(key_grads[WINDOW:])
            gain_total = gain_total + gain_grad
        return (produced, grad_total[WINDOW:].astype(jnp.bfloat16), gain_total)
    produced, row_grads, gain_grad = lax.map(one_pair, (section_input.reshape(pair_count, SEQ_LEN, FEATURES), section_positions.reshape(pair_count, SEQ_LEN), saved_input.reshape(pair_count, SEQ_LEN, FEATURES), saved_positions.reshape(pair_count, SEQ_LEN), cotangent.reshape(pair_count, SEQ_LEN, FEATURES), jnp.arange(pair_count, dtype=jnp.int32)))
    produced = produced.reshape(N_DP, N_PIPE, SEQ_LEN, FEATURES)
    row_grads = row_grads.reshape(N_DP, N_PIPE, SEQ_LEN, FEATURES)
    next_input = jnp.roll(produced, 1, axis=1)
    upstream_grad = jnp.roll(row_grads, -1, axis=1)
    gain_grads = lax.optimization_barrier(jnp.sum(gain_grad.reshape(N_DP, N_PIPE, 3, FEATURES), axis=0)) / jnp.float32(TOK_DEV)
    return (next_input, upstream_grad, gain_grads)
```

```python
import functools

import jax
import jax.numpy as jnp
from jax import lax
from jax.experimental import pallas as pl
from jax.experimental.pallas import tpu as pltpu
from jax.sharding import PartitionSpec as P

HEADS = 16
HEAD_DIM = 128
FEATURES = 2048
WINDOW = 512
TOK = 128
PAIR = 2 * TOK
SPAN = WINDOW + PAIR
SLOTS = HEADS // 2
AHEAD = 2
EPSILON = 1e-06
SCALE = HEAD_DIM**-0.5
MESH = pl.DeviceIdType.MESH
F32 = jnp.float32
BF16 = jnp.bfloat16
FAR, NEAR, OWN = 0, PAIR, 2 * PAIR


def sum_stages(sizes):
    stages = []
    for axis, left, stride in (("dp", sizes["dp"], 1), ("ctx", sizes["ctx"] // 2, 2)):
        while left > 1:
            factor = next(f for f in range(2, left + 1) if left % f == 0)
            stages.append((axis, stride, factor))
            left //= factor
            stride *= factor
    return stages


def dot(left, right, left_dim, right_dim):
    return lax.dot_general(
        left, right, (((left_dim,), (right_dim,)), ((), ())), preferred_element_type=F32
    )


def kernel(
    sizes,
    sec_ref,
    sec_pos,
    sav_ref,
    sav_pos,
    cot_ref,
    norm_ref,
    outg_ref,
    plan_ref,
    next_ref,
    up_ref,
    total_ref,
    keys,
    cot,
    pos,
    norm_in,
    outg_in,
    plan_in,
    gains,
    masks,
    grads,
    own,
    from_near,
    from_far,
    produced,
    dx,
    sums,
    halves,
    load_sem,
    small_sem,
    pos_sem,
    swap_recv,
    cot_recv,
    pair_recv,
    relay_recv,
    near_recv,
    far_recv,
    out_recv,
    send_sem,
    sum_send,
    sum_recv,
):
    n = sizes["ctx"]
    c = lax.axis_index("ctx")
    side = lax.rem(c, 2)
    partner = c + 1 - 2 * side
    pipe = lax.axis_index("pipe")
    after = lax.rem(pipe + 1, sizes["pipe"])
    before = lax.rem(pipe + sizes["pipe"] - 1, sizes["pipe"])
    up, down = c + 2 < n, c >= 2
    up2, down2 = c + 4 < n, c >= 4
    stages = sum_stages(sizes)
    SWAP, COT, POS, PAIRS, RELAY, NEARG, FARG, OUT, HALF = range(9)

    def part(first, which):
        return pl.ds(pl.multiple_of(first + which * TOK, TOK), TOK)

    def lanes_of(h):
        return pl.ds(pl.multiple_of(h * HEAD_DIM, HEAD_DIM), HEAD_DIM)

    def remote(source, target, send, recv, device):
        return pltpu.make_async_remote_copy(
            src_ref=source,
            dst_ref=target,
            send_sem=send,
            recv_sem=recv,
            device_id=device,
            device_id_type=MESH,
        )

    def wait_bytes(ref, sem):
        pltpu.make_async_copy(ref, ref, sem).wait()

    def load(which, j):
        source = (sav_ref, sec_ref, cot_ref)[which]
        mine = part(0, side) if which == 2 else part(OWN, side)
        target = cot.at[j, mine] if which == 2 else keys.at[which, j, mine]
        return pltpu.make_async_copy(
            source.at[:, lanes_of(side * SLOTS + j)], target, load_sem.at[which]
        )

    def swap_copy(t, j):
        mine = part(OWN, side)
        return remote(
            (sav_ref, sec_ref)[t].at[:, lanes_of((1 - side) * SLOTS + j)],
            keys.at[t, j, mine],
            send_sem.at[SWAP],
            swap_recv.at[t * SLOTS + j],
            {"ctx": partner},
        )

    def cot_copy(j):
        return remote(
            cot_ref.at[:, lanes_of((1 - side) * SLOTS + j)],
            cot.at[j, part(0, side)],
            send_sem.at[COT],
            cot_recv.at[j],
            {"ctx": partner},
        )

    def pos_copy(t):
        return remote(
            (sav_pos, sec_pos)[t],
            pos.at[t, side],
            send_sem.at[POS],
            pos_sem.at[1],
            {"ctx": partner},
        )

    def pair_copy(s, which):
        t, j = s // SLOTS, lax.rem(s, SLOTS)
        return remote(
            keys.at[t, j, part(OWN, which)],
            keys.at[t, j, part(NEAR, which)],
            send_sem.at[PAIRS],
            pair_recv.at[s],
            {"ctx": c + 2},
        )

    def relay_copy(s):
        t, j = s // SLOTS, lax.rem(s, SLOTS)
        return remote(
            keys.at[t, j, pl.ds(NEAR, PAIR)],
            keys.at[t, j, pl.ds(FAR, PAIR)],
            send_sem.at[RELAY],
            relay_recv.at[s],
            {"ctx": c + 2},
        )

    def near_copy(j):
        return remote(
            grads.at[j, pl.ds(NEAR, PAIR)],
            from_near.at[j],
            send_sem.at[NEARG],
            near_recv.at[j],
            {"ctx": c - 2},
        )

    def far_copy(j):
        return remote(
            grads.at[j, pl.ds(FAR, PAIR)],
            from_far.at[j],
            send_sem.at[FARG],
            far_recv.at[j],
            {"ctx": c - 4},
        )

    def out_copy(kind, j, which):
        device = {"pipe": (after, before)[kind]}
        if which == 1:
            device["ctx"] = partner
        rows = part(0, side if which == 0 else 1 - side)
        return remote(
            (produced, dx)[kind].at[j, rows],
            (next_ref, up_ref)[kind].at[:, lanes_of(side * SLOTS + j)],
            send_sem.at[OUT + kind],
            out_recv.at[kind],
            device,
        )

    def digit_of(stage):
        axis, stride, factor = stages[stage]
        return lax.rem(lax.axis_index(axis) // stride, factor)

    def sum_peer(stage, offset):
        axis, stride, factor = stages[stage]
        digit = digit_of(stage)
        return {axis: lax.axis_index(axis) + (lax.rem(digit + offset, factor) - digit) * stride}

    def sum_copy(stage, offset, sender):
        return remote(
            sums.at[stage, digit_of(stage)],
            sums.at[stage, sender],
            sum_send.at[stage, offset - 1],
            sum_recv.at[stage, offset - 1],
            sum_peer(stage, offset),
        )

    def half_copy():
        return remote(
            halves.at[side],
            halves.at[side],
            pos_sem.at[2],
            pos_sem.at[3],
            {"ctx": partner},
        )

    def start_sum(stage):
        for offset in range(1, stages[stage][2]):
            sum_copy(stage, offset, digit_of(stage)).start()

    def finish_sum(stage):
        factor = stages[stage][2]
        for offset in range(1, factor):
            sender = lax.rem(digit_of(stage) + factor - offset, factor)
            sum_copy(stage, offset, sender).wait_recv()
        total = sums[stage, 0]
        for digit in range(1, factor):
            total = total + sums[stage, digit]
        if stage + 1 < len(stages):
            sums[stage + 1, digit_of(stage + 1)] = total
            start_sum(stage + 1)
        else:
            finish_half(total)

    def finish_half(total):
        halves[side] = total * (1.0 / TOK)
        half_copy().start()

    def finish_total():
        half_copy().wait_recv()
        for which in range(2):
            for m in range(3):
                total_ref[pl.ds(m * HEADS + which * SLOTS, SLOTS), :] = halves[
                    which, pl.ds(m * SLOTS, SLOTS), :
                ]

    def step_sum(step):
        if step < len(stages):
            finish_sum(step)
        elif step == len(stages):
            finish_total()

    def each(action):
        @pl.loop(0, SLOTS)
        def _(j):
            action(j)

    barrier = pltpu.get_barrier_semaphore()

    def greet(device):
        pl.semaphore_signal(barrier, inc=1, device_id=device, device_id_type=MESH)

    greet({"ctx": partner})
    greet({"pipe": after})
    greet({"ctx": partner, "pipe": after})
    count = 3
    if sizes["pipe"] > 2:
        greet({"pipe": before})
        greet({"ctx": partner, "pipe": before})
        count += 2
    for condition, device in ((up, c + 2), (down, c - 2), (up2, c + 4), (down2, c - 4)):
        pl.when(condition)(lambda: greet({"ctx": device}))
        count = count + condition.astype(jnp.int32)
    for stage, (axis, stride, factor) in enumerate(stages):
        if axis == "ctx" and factor == 2 and stride <= 4:
            continue
        for offset in range(1, factor):
            greet(sum_peer(stage, offset))
            count += 1

    each(lambda j: load(0, j).start())
    small = (
        (norm_ref, norm_in),
        (outg_ref, outg_in),
        (plan_ref, plan_in),
        (sav_pos, pos.at[0, side]),
        (sec_pos, pos.at[1, side]),
    )
    for i, (source, target) in enumerate(small):
        pltpu.make_async_copy(source, target, small_sem.at[i]).start()
    each(lambda j: load(2, j).start())
    each(lambda j: load(1, j).start())
    wait_bytes(keys.at[0, :, pl.ds(0, TOK)], load_sem.at[0])
    pl.semaphore_wait(barrier, count)

    def pass_pair(s, which):
        pl.when(up)(lambda: pair_copy(s, which).start())

    def relay(s):
        @pl.when(down)
        def _():
            wait_bytes(keys.at[0, 0, pl.ds(NEAR, PAIR)], pair_recv.at[s])
            pl.when(up)(lambda: relay_copy(s).start())

    def wait_swap(s):
        wait_bytes(keys.at[0, 0, pl.ds(0, TOK)], swap_recv.at[s])

    for t in range(2):
        pos_copy(t).start()

    def first_swaps(j):
        swap_copy(0, j).start()
        pl.when(j < AHEAD)(lambda: pass_pair(j, side))
        cot_copy(j).start()

    each(first_swaps)
    each(lambda j: swap_copy(1, j).start())

    for i, (source, target) in enumerate(small):
        pltpu.make_async_copy(source, target, small_sem.at[i]).wait()
    for which in range(2):
        lap = plan_in[0, which]
        gains[pl.ds(3 * which, 2), :] = jnp.where(lap == 1, norm_in[1], norm_in[0])
        gains[pl.ds(3 * which + 2, 1), :] = jnp.where(lap == 1, outg_in[1], outg_in[0])
    for reach, first in ((2, NEAR), (4, FAR)):

        @pl.when(c < reach)
        def _():
            @pl.loop(0, SLOTS)
            def _(j):
                for t in range(2):
                    keys[t, j, pl.ds(first, PAIR)] = jnp.zeros((PAIR, HEAD_DIM), BF16)

    for s in range(AHEAD):
        wait_swap(s)
        pass_pair(s, 1 - side)

    wait_bytes(pos.at[:, 0], pos_sem.at[1])
    distance = (
        lax.broadcasted_iota(jnp.int32, (SPAN, TOK), 1)
        + WINDOW
        - lax.broadcasted_iota(jnp.int32, (SPAN, TOK), 0)
    )
    for t in range(2):
        for which in range(2):
            apart = distance + which * TOK
            allowed = (apart >= 0) & (apart < WINDOW) & (apart <= pos[t, which])
            masks[t, :, pl.ds(which * TOK, TOK)] = jnp.where(allowed, 1.0, 0.0).astype(F32)

    wait_bytes(cot.at[:, pl.ds(0, TOK)], load_sem.at[2])
    wait_bytes(keys.at[1, :, pl.ds(0, TOK)], load_sem.at[1])
    relay(0)

    def normed(x):
        wide = x.astype(F32)
        inverse = lax.rsqrt(jnp.mean(wide * wide, axis=-1, keepdims=True) + EPSILON)
        return wide * inverse, inverse

    def weights(t, n_all, a, b):
        k = (n_all * b).astype(BF16)
        q = (n_all[WINDOW:] * a).astype(BF16)
        w = jnp.exp(dot(k, q, 1, 1) * SCALE) * masks[t]
        prob = w * (1.0 / jnp.sum(w, axis=0, keepdims=True))
        return q, k, prob

    sum_slot = digit_of(0) if stages else 0

    def backward(j):
        wide = lanes_of(side * SLOTS + j)
        a, b, g = (gains[pl.ds(3 + m, 1), wide] for m in range(3))
        x = keys[0, j]
        n_all, inverse = normed(x)
        q, k, prob = weights(0, n_all, a, b)
        p = prob.astype(BF16)
        ct = cot[j].astype(F32)
        d_mix = (ct * g).astype(BF16)
        d_prob = dot(x, d_mix, 1, 1)
        delta = jnp.sum(prob * d_prob, axis=0, keepdims=True)
        d_score = (prob * (d_prob - delta)).astype(BF16)
        mix = dot(p, x, 0, 0)
        d_k = dot(d_score, q, 1, 0)
        d_q = dot(d_score, k, 0, 0)
        d_value = dot(p, d_mix, 1, 0)
        n_own = n_all[WINDOW:]
        d_n = d_k * (b * SCALE)
        d_n_own = d_n[WINDOW:] + d_q * (a * SCALE)

        def through_norm(d, value, scale):
            return scale * (d - value * jnp.mean(d * value, axis=-1, keepdims=True))

        grads[j] = (
            d_value[:WINDOW] + through_norm(d_n[:WINDOW], n_all[:WINDOW], inverse[:WINDOW])
        ).astype(BF16)
        own[j] = d_value[WINDOW:] + through_norm(d_n_own, n_own, inverse[WINDOW:]) + ct
        parts = (
            jnp.sum(d_q * n_own, axis=0, keepdims=True) * SCALE,
            jnp.sum(d_k * n_all, axis=0, keepdims=True) * SCALE,
            jnp.sum(ct * mix, axis=0, keepdims=True),
        )
        for m in range(3):
            sums[0, sum_slot, pl.ds(m * SLOTS + j, 1), :] = parts[m]

    def forward(j):
        wide = lanes_of(side * SLOTS + j)
        a, b, g = (gains[pl.ds(m, 1), wide] for m in range(3))
        x = keys[1, j]
        n_all, _ = normed(x)
        _, _, prob = weights(1, n_all, a, b)
        mix = dot(prob.astype(BF16), x, 0, 0)
        produced[j] = (x[WINDOW:].astype(F32) + g * mix).astype(BF16)

    def feed(s, total):
        @pl.when(s + AHEAD < total)
        def _():
            wait_swap(s + AHEAD)
            pass_pair(s + AHEAD, side)
            pass_pair(s + AHEAD, 1 - side)

        pl.when(s + 1 < total)(lambda: relay(s + 1))
        pl.when(down2)(lambda: wait_bytes(keys.at[0, 0, pl.ds(FAR, PAIR)], relay_recv.at[s]))

    def first(j):
        feed(j, 2 * SLOTS)
        wait_bytes(cot.at[0, pl.ds(0, TOK)], cot_recv.at[j])
        backward(j)
        pl.when(down)(lambda: near_copy(j).start())
        pl.when(down2)(lambda: far_copy(j).start())

    each(first)
    if stages:
        start_sum(0)
    else:
        finish_half(sums[0, 0])

    def send_dx(j):
        @pl.when(up)
        def _():
            near_copy(j).wait_recv()
            own[j] = own[j] + from_near[j].astype(F32)

        @pl.when(up2)
        def _():
            far_copy(j).wait_recv()
            own[j] = own[j] + from_far[j].astype(F32)

        dx[j] = own[j].astype(BF16)
        for which in range(2):
            out_copy(1, j, which).start()

    def last(j):
        feed(j + SLOTS, 2 * SLOTS)
        forward(j)
        for which in range(2):
            out_copy(0, j, which).start()
        for step in range(min(SLOTS, len(stages) + 1)):
            pl.when(j == step)(lambda: step_sum(step))
        send_dx(j)

    each(last)
    for step in range(SLOTS, len(stages) + 1):
        step_sum(step)

    swapped = keys.at[:, :, pl.ds(0, TOK)]
    paired = keys.at[:, :, pl.ds(0, PAIR)]
    wait_bytes(swapped, send_sem.at[SWAP])
    wait_bytes(cot.at[:, pl.ds(0, TOK)], send_sem.at[COT])
    wait_bytes(pos.at[:, 0], send_sem.at[POS])
    pl.when(up)(lambda: wait_bytes(paired, send_sem.at[PAIRS]))
    pl.when(up & down)(lambda: wait_bytes(paired, send_sem.at[RELAY]))
    pl.when(down)(lambda: wait_bytes(from_near, send_sem.at[NEARG]))
    pl.when(down2)(lambda: wait_bytes(from_far, send_sem.at[FARG]))
    half_copy().wait_send()
    for stage, (_, _, factor) in enumerate(stages):
        for offset in range(1, factor):
            sum_copy(stage, offset, digit_of(stage)).wait_send()
    for kind, (sent, target) in enumerate(((produced, next_ref), (dx, up_ref))):
        wait_bytes(sent, send_sem.at[OUT + kind])
        wait_bytes(target, out_recv.at[kind])


def local(
    sizes,
    section_input,
    section_positions,
    saved_input,
    saved_positions,
    cotangent,
    norm_gains,
    output_gains,
    plan,
):
    stages = sum_stages(sizes)
    widest = max([factor for _, _, factor in stages] + [2])
    depth = max(len(stages), 1)
    anywhere = pl.BlockSpec(memory_space=pl.ANY)
    in_vmem = pl.BlockSpec(memory_space=pltpu.VMEM)
    produced, grads, totals = pl.pallas_call(
        functools.partial(kernel, sizes),
        out_shape=(
            jax.ShapeDtypeStruct((TOK, FEATURES), BF16),
            jax.ShapeDtypeStruct((TOK, FEATURES), BF16),
            jax.ShapeDtypeStruct((3 * HEADS, HEAD_DIM), F32),
        ),
        in_specs=[anywhere] * 8,
        out_specs=(anywhere, anywhere, in_vmem),
        scratch_shapes=[
            pltpu.VMEM((2, SLOTS, SPAN, HEAD_DIM), BF16),
            pltpu.VMEM((SLOTS, PAIR, HEAD_DIM), BF16),
            pltpu.VMEM((2, 2, 1, TOK), jnp.int32),
            pltpu.VMEM((2, 2, FEATURES), F32),
            pltpu.VMEM((2, 1, FEATURES), F32),
            pltpu.SMEM((1, 2), jnp.int32),
            pltpu.VMEM((8, FEATURES), F32),
            pltpu.VMEM((2, SPAN, PAIR), F32),
            pltpu.VMEM((SLOTS, WINDOW, HEAD_DIM), BF16),
            pltpu.VMEM((SLOTS, PAIR, HEAD_DIM), F32),
            pltpu.VMEM((SLOTS, PAIR, HEAD_DIM), BF16),
            pltpu.VMEM((SLOTS, PAIR, HEAD_DIM), BF16),
            pltpu.VMEM((SLOTS, PAIR, HEAD_DIM), BF16),
            pltpu.VMEM((SLOTS, PAIR, HEAD_DIM), BF16),
            pltpu.VMEM((depth, widest, 3 * SLOTS, HEAD_DIM), F32),
            pltpu.VMEM((2, 3 * SLOTS, HEAD_DIM), F32),
            pltpu.SemaphoreType.DMA((3,)),
            pltpu.SemaphoreType.DMA((5,)),
            pltpu.SemaphoreType.DMA((4,)),
            pltpu.SemaphoreType.DMA((2 * SLOTS,)),
            pltpu.SemaphoreType.DMA((SLOTS,)),
            pltpu.SemaphoreType.DMA((2 * SLOTS,)),
            pltpu.SemaphoreType.DMA((2 * SLOTS,)),
            pltpu.SemaphoreType.DMA((SLOTS,)),
            pltpu.SemaphoreType.DMA((SLOTS,)),
            pltpu.SemaphoreType.DMA((2,)),
            pltpu.SemaphoreType.DMA((9,)),
            pltpu.SemaphoreType.DMA((depth, widest - 1)),
            pltpu.SemaphoreType.DMA((depth, widest - 1)),
        ],
        compiler_params=pltpu.CompilerParams(
            collective_id=0, has_side_effects=True, vmem_limit_bytes=24 * 1024 * 1024
        ),
        cost_estimate=pl.CostEstimate(
            flops=9 * 2 * TOK * SPAN * FEATURES,
            bytes_accessed=5 * TOK * FEATURES * 2,
            transcendentals=2 * HEADS * TOK * SPAN,
        ),
    )(
        section_input[0, 0],
        section_positions[0],
        saved_input[0, 0],
        saved_positions[0],
        cotangent[0, 0],
        norm_gains[:, 0],
        output_gains,
        plan[0],
    )
    return (produced[None, None], grads[None, None], totals.reshape(1, 3, FEATURES))


def solution(mesh):
    placed = (
        P("dp", "pipe", "ctx", None),
        P("dp", "pipe", "ctx"),
        P("dp", "pipe", "ctx", None),
        P("dp", "pipe", "ctx"),
        P("dp", "pipe", "ctx", None),
        P(None, "pipe", None, None),
        P(None, "pipe", None),
        P("dp", "pipe", None),
    )
    return jax.shard_map(
        functools.partial(local, {axis: mesh.shape[axis] for axis in ("dp", "pipe", "ctx")}),
        mesh=mesh,
        in_specs=placed,
        out_specs=(
            P("dp", "pipe", "ctx", None),
            P("dp", "pipe", "ctx", None),
            P("pipe", None, None),
        ),
        check_vma=False,
    )
```

```python
import functools

import jax
import jax.numpy as jnp
from jax import lax
from jax.experimental import pallas as pl
from jax.experimental.pallas import tpu as pltpu
from jax.sharding import PartitionSpec as P

HEADS = 16
HEAD_DIM = 128
FEATURES = 2048
WINDOW = 512
TOK = 128
PAIR = 2 * TOK
SPAN = WINDOW + PAIR
SLOTS = HEADS // 2
OWN_AHEAD = 5
AHEAD = 3
PASS = 2
DELAY = 4
EPSILON = 1e-06
SCALE = HEAD_DIM**-0.5
LOG2E = 1.4426950408889634
MESH = pl.DeviceIdType.MESH
F32 = jnp.float32
BF16 = jnp.bfloat16
FAR, NEAR, OWN = 0, PAIR, 2 * PAIR


def sum_stages(sizes):
    stages = []
    left, stride = sizes["dp"], 1
    while left > 1:
        factor = next(f for f in range(2, left + 1) if left % f == 0)
        stages.append(("dp", stride, factor))
        left //= factor
        stride *= factor
    return stages


def dot(left, right, left_dim, right_dim):
    return lax.dot_general(
        left, right, (((left_dim,), (right_dim,)), ((), ())), preferred_element_type=F32
    )


def kernel(
    sizes,
    sec_ref,
    sec_pos,
    sav_ref,
    sav_pos,
    cot_ref,
    norm_ref,
    outg_ref,
    plan_ref,
    next_ref,
    up_ref,
    total_ref,
    keys,
    cot,
    pos,
    norm_in,
    outg_in,
    plan_in,
    gains,
    masks,
    grads,
    own,
    from_near,
    from_far,
    produced,
    dx,
    sums,
    columns,
    halves,
    load_sem,
    small_sem,
    pos_sem,
    swap_recv,
    cot_recv,
    pair_recv,
    relay_recv,
    near_recv,
    far_recv,
    out_recv,
    send_sem,
    sum_send,
    sum_recv,
    column_recv,
):
    n = sizes["ctx"]
    c = lax.axis_index("ctx")
    side = lax.rem(c, 2)
    partner = c + 1 - 2 * side
    pipe = lax.axis_index("pipe")
    after = lax.rem(pipe + 1, sizes["pipe"])
    before = lax.rem(pipe + sizes["pipe"] - 1, sizes["pipe"])
    up, down = c + 2 < n, c >= 2
    down2 = c >= 4
    level, levels = c // 2, n // 2
    stages = sum_stages(sizes)
    SWAP, COT, POS, PAIRS, RELAY, NEARG, FARG, OUT = range(8)

    def part(first, which):
        return pl.ds(pl.multiple_of(first + which * TOK, TOK), TOK)

    def lanes_of(h):
        return pl.ds(pl.multiple_of(h * HEAD_DIM, HEAD_DIM), HEAD_DIM)

    def remote(source, target, send, recv, device):
        return pltpu.make_async_remote_copy(
            src_ref=source,
            dst_ref=target,
            send_sem=send,
            recv_sem=recv,
            device_id=device,
            device_id_type=MESH,
        )

    def wait_bytes(ref, sem):
        pltpu.make_async_copy(ref, ref, sem).wait()

    def load(which, j):
        source = (sav_ref, sec_ref, cot_ref)[which]
        mine = part(0, side) if which == 2 else part(OWN, side)
        target = cot.at[j, mine] if which == 2 else keys.at[which, j, mine]
        return pltpu.make_async_copy(
            source.at[:, lanes_of(side * SLOTS + j)], target, load_sem.at[which]
        )

    def swap_copy(t, j):
        mine = part(OWN, side)
        return remote(
            (sav_ref, sec_ref)[t].at[:, lanes_of((1 - side) * SLOTS + j)],
            keys.at[t, j, mine],
            send_sem.at[SWAP],
            swap_recv.at[t * SLOTS + j],
            {"ctx": partner},
        )

    def cot_copy(j):
        return remote(
            cot_ref.at[:, lanes_of((1 - side) * SLOTS + j)],
            cot.at[j, part(0, side)],
            send_sem.at[COT],
            cot_recv.at[j],
            {"ctx": partner},
        )

    def pos_copy(t):
        return remote(
            (sav_pos, sec_pos)[t],
            pos.at[t, side],
            send_sem.at[POS],
            pos_sem.at[1],
            {"ctx": partner},
        )

    def pair_copy(s, which):
        t, j = s // SLOTS, lax.rem(s, SLOTS)
        return remote(
            keys.at[t, j, part(OWN, which)],
            keys.at[t, j, part(NEAR, which)],
            send_sem.at[PAIRS],
            pair_recv.at[s],
            {"ctx": c + 2},
        )

    def relay_copy(s):
        t, j = s // SLOTS, lax.rem(s, SLOTS)
        return remote(
            keys.at[t, j, pl.ds(NEAR, PAIR)],
            keys.at[t, j, pl.ds(FAR, PAIR)],
            send_sem.at[RELAY],
            relay_recv.at[s],
            {"ctx": c + 2},
        )

    def near_copy(j):
        return remote(
            grads.at[j, pl.ds(NEAR, PAIR)],
            from_near.at[j],
            send_sem.at[NEARG],
            near_recv.at[j],
            {"ctx": c - 2},
        )

    def far_copy(j):
        return remote(
            grads.at[j, pl.ds(FAR, PAIR)],
            from_far.at[j],
            send_sem.at[FARG],
            far_recv.at[j],
            {"ctx": c - 2},
        )

    def out_copy(kind, j, which):
        device = {"pipe": (after, before)[kind]}
        if which == 1:
            device["ctx"] = partner
        rows = part(0, side if which == 0 else 1 - side)
        return remote(
            (produced, dx)[kind].at[j, rows],
            (next_ref, up_ref)[kind].at[:, lanes_of(side * SLOTS + j)],
            send_sem.at[OUT + kind],
            out_recv.at[kind],
            device,
        )

    def digit_of(stage):
        axis, stride, factor = stages[stage]
        return lax.rem(lax.axis_index(axis) // stride, factor)

    def sum_peer(stage, offset):
        axis, stride, factor = stages[stage]
        digit = digit_of(stage)
        return {axis: lax.axis_index(axis) + (lax.rem(digit + offset, factor) - digit) * stride}

    def sum_copy(stage, offset, sender):
        return remote(
            sums.at[stage, digit_of(stage)],
            sums.at[stage, sender],
            sum_send.at[stage, offset - 1],
            sum_recv.at[stage, offset - 1],
            sum_peer(stage, offset),
        )

    def half_copy():
        return remote(
            halves.at[side],
            halves.at[side],
            pos_sem.at[2],
            pos_sem.at[3],
            {"ctx": partner},
        )

    def start_sum(stage):
        for offset in range(1, stages[stage][2]):
            sum_copy(stage, offset, digit_of(stage)).start()

    def finish_sum(stage):
        factor = stages[stage][2]
        for offset in range(1, factor):
            sender = lax.rem(digit_of(stage) + factor - offset, factor)
            sum_copy(stage, offset, sender).wait_recv()
        total = sums[stage, 0]
        for digit in range(1, factor):
            total = total + sums[stage, digit]
        if stage + 1 < len(stages):
            sums[stage + 1, digit_of(stage + 1)] = total
            start_sum(stage + 1)
        else:
            start_column(total)

    def column_copy(which, step):
        return remote(
            columns.at[which],
            columns.at[which],
            pos_sem.at[4],
            column_recv.at[which],
            {"ctx": c + step},
        )

    def start_column(total):
        columns[level] = total
        pl.when(up)(lambda: column_copy(level, 2).start())
        pl.when(down)(lambda: column_copy(level, -2).start())

    def pass_column(k):
        below, above = level - k, level + k

        @pl.when(below >= 0)
        def _():
            wait_bytes(columns.at[0], column_recv.at[below])
            pl.when(up)(lambda: column_copy(below, 2).start())

        @pl.when(above < levels)
        def _():
            wait_bytes(columns.at[0], column_recv.at[above])
            pl.when(down)(lambda: column_copy(above, -2).start())

    def finish_column():
        total = columns[0]
        for which in range(1, levels):
            total = total + columns[which]
        finish_half(total)

    def finish_half(total):
        halves[side] = total * (1.0 / TOK)
        half_copy().start()

    def finish_total():
        half_copy().wait_recv()
        for which in range(2):
            for m in range(3):
                total_ref[pl.ds(m * HEADS + which * SLOTS, SLOTS), :] = halves[
                    which, pl.ds(m * SLOTS, SLOTS), :
                ]

    steps = [functools.partial(finish_sum, stage) for stage in range(len(stages))]
    steps += [functools.partial(pass_column, k) for k in range(1, levels)]

    def last_column():
        pass_column(levels - 1)
        finish_column()

    steps[-1] = last_column
    steps.append(finish_total)

    def each(action):
        @pl.loop(0, SLOTS)
        def _(j):
            action(j)

    barrier = pltpu.get_barrier_semaphore()

    def greet(device):
        pl.semaphore_signal(barrier, inc=1, device_id=device, device_id_type=MESH)

    greet({"ctx": partner})
    greet({"pipe": after})
    greet({"ctx": partner, "pipe": after})
    count = 3
    if sizes["pipe"] > 2:
        greet({"pipe": before})
        greet({"ctx": partner, "pipe": before})
        count += 2
    for condition, device in ((up, c + 2), (down, c - 2)):
        pl.when(condition)(lambda: greet({"ctx": device}))
        count = count + condition.astype(jnp.int32)
    for stage, (_, _, factor) in enumerate(stages):
        for offset in range(1, factor):
            greet(sum_peer(stage, offset))
            count += 1

    each(lambda j: load(0, j).start())
    small = (
        (norm_ref, norm_in),
        (outg_ref, outg_in),
        (plan_ref, plan_in),
        (sav_pos, pos.at[0, side]),
        (sec_pos, pos.at[1, side]),
    )
    for i, (source, target) in enumerate(small):
        pltpu.make_async_copy(source, target, small_sem.at[i]).start()
    each(lambda j: load(2, j).start())
    each(lambda j: load(1, j).start())
    wait_bytes(keys.at[0, :, pl.ds(0, TOK)], load_sem.at[0])
    pl.semaphore_wait(barrier, count)

    def pass_pair(s, which):
        pl.when(up)(lambda: pair_copy(s, which).start())

    def relay(s):
        @pl.when(down)
        def _():
            wait_bytes(keys.at[0, 0, pl.ds(NEAR, PAIR)], pair_recv.at[s])
            pl.when(up)(lambda: relay_copy(s).start())

    def wait_swap(s):
        wait_bytes(keys.at[0, 0, pl.ds(0, TOK)], swap_recv.at[s])

    for t in range(2):
        pos_copy(t).start()

    def first_swaps(j):
        swap_copy(0, j).start()
        pl.when(j < OWN_AHEAD)(lambda: pass_pair(j, side))
        cot_copy(j).start()

    each(first_swaps)
    each(lambda j: swap_copy(1, j).start())

    for i, (source, target) in enumerate(small):
        pltpu.make_async_copy(source, target, small_sem.at[i]).wait()
    for which in range(2):
        lap = plan_in[0, which]
        gains[pl.ds(3 * which, 2), :] = jnp.where(lap == 1, norm_in[1], norm_in[0])
        gains[pl.ds(3 * which + 2, 1), :] = jnp.where(lap == 1, outg_in[1], outg_in[0])
    for reach, first in ((2, NEAR), (4, FAR)):

        @pl.when(c < reach)
        def _():
            @pl.loop(0, SLOTS)
            def _(j):
                for t in range(2):
                    keys[t, j, pl.ds(first, PAIR)] = jnp.zeros((PAIR, HEAD_DIM), BF16)

    for s in range(AHEAD):
        wait_swap(s)
        pass_pair(s, 1 - side)

    wait_bytes(pos.at[:, 0], pos_sem.at[1])
    distance = (
        lax.broadcasted_iota(jnp.int32, (SPAN, TOK), 1)
        + WINDOW
        - lax.broadcasted_iota(jnp.int32, (SPAN, TOK), 0)
    )
    for t in range(2):
        for which in range(2):
            apart = distance + which * TOK
            allowed = (apart >= 0) & (apart < WINDOW) & (apart <= pos[t, which])
            masks[t, :, pl.ds(which * TOK, TOK)] = jnp.where(allowed, 1.0, 0.0).astype(F32)

    wait_bytes(cot.at[:, pl.ds(0, TOK)], load_sem.at[2])
    wait_bytes(keys.at[1, :, pl.ds(0, TOK)], load_sem.at[1])
    for s in range(PASS):
        relay(s)

    def normed(x):
        wide = x.astype(F32)
        inverse = lax.rsqrt(jnp.mean(wide * wide, axis=-1, keepdims=True) + EPSILON)
        return wide * inverse, inverse

    def probability(t, k, q, queries):
        w = jnp.exp2(dot(k, q, 1, 1) * (SCALE * LOG2E)) * masks[t, :, queries]
        return w * (1.0 / jnp.sum(w, axis=0, keepdims=True))

    sum_slot = digit_of(0) if stages else 0

    def backward(j):
        wide = lanes_of(side * SLOTS + j)
        a, b, g = (gains[pl.ds(3 + m, 1), wide] for m in range(3))
        x = keys[0, j]
        n_all, inverse = normed(x)
        k = (n_all * b).astype(BF16)
        q = (n_all[WINDOW:] * a).astype(BF16)
        prob = probability(0, k, q, pl.ds(0, PAIR))
        p = prob.astype(BF16)
        ct = cot[j].astype(F32)
        d_mix = (ct * g).astype(BF16)
        d_prob = dot(x, d_mix, 1, 1)
        delta = jnp.sum(prob * d_prob, axis=0, keepdims=True)
        d_score = (prob * (d_prob - delta)).astype(BF16)
        d_k = dot(d_score, q, 1, 0)
        d_q = dot(k, d_score, 0, 0).T
        mixed = dot(p, cot[j], 1, 0)
        d_value = mixed * g
        n_own = n_all[WINDOW:]
        d_n = d_k * (b * SCALE)
        d_n_own = d_n[WINDOW:] + d_q * (a * SCALE)

        def through_norm(d, value, scale):
            return scale * (d - value * jnp.mean(d * value, axis=-1, keepdims=True))

        grads[j] = (
            d_value[:WINDOW] + through_norm(d_n[:WINDOW], n_all[:WINDOW], inverse[:WINDOW])
        ).astype(BF16)
        own[j] = d_value[WINDOW:] + through_norm(d_n_own, n_own, inverse[WINDOW:]) + ct
        parts = (
            jnp.sum(d_q * n_own, axis=0, keepdims=True) * SCALE,
            jnp.sum(d_k * n_all, axis=0, keepdims=True) * SCALE,
            jnp.sum(mixed * x, axis=0, keepdims=True),
        )
        for m in range(3):
            sums[0, sum_slot, pl.ds(m * SLOTS + j, 1), :] = parts[m]

    def forward(j):
        wide = lanes_of(side * SLOTS + j)
        a, b, g = (gains[pl.ds(m, 1), wide] for m in range(3))
        x = keys[1, j]
        k = (normed(x)[0] * b).astype(BF16)
        for which in (1, 0):
            rows = side if which == 0 else 1 - side
            mine = keys[1, j, part(OWN, rows)]
            q = (normed(mine)[0] * a).astype(BF16)
            prob = probability(1, k, q, part(0, rows))
            mix = dot(x, prob.astype(BF16), 0, 0).T
            produced[j, part(0, rows)] = (mine.astype(F32) + g * mix).astype(BF16)
            out_copy(0, j, which).start()

    def feed(s, total):
        @pl.when(s + AHEAD < total)
        def _():
            wait_swap(s + AHEAD)
            pass_pair(s + AHEAD, 1 - side)

        pl.when(s + OWN_AHEAD < total)(lambda: pass_pair(s + OWN_AHEAD, side))

        pl.when(s + PASS < total)(lambda: relay(s + PASS))
        pl.when(down2)(lambda: wait_bytes(keys.at[0, 0, pl.ds(FAR, PAIR)], relay_recv.at[s]))

    def send_near(j):
        @pl.when(up & down)
        def _():
            far_copy(j).wait_recv()
            near = grads[j, pl.ds(NEAR, PAIR)].astype(F32) + from_far[j].astype(F32)
            grads[j, pl.ds(NEAR, PAIR)] = near.astype(BF16)
            near_copy(j).start()

    def first(j):
        feed(j, 2 * SLOTS)
        wait_bytes(cot.at[0, pl.ds(0, TOK)], cot_recv.at[j])
        backward(j)
        pl.when(down2)(lambda: far_copy(j).start())
        pl.when(down & jnp.logical_not(up))(lambda: near_copy(j).start())
        pl.when(j >= DELAY)(lambda: send_near(jnp.maximum(j - DELAY, 0)))

    each(first)
    if stages:
        start_sum(0)
    else:
        start_column(sums[0, 0])

    def send_dx(j):
        @pl.when(up)
        def _():
            near_copy(j).wait_recv()
            own[j] = own[j] + from_near[j].astype(F32)

        dx[j] = own[j].astype(BF16)
        for which in range(2):
            out_copy(1, j, which).start()

    def last(j):
        pl.when(j < DELAY)(lambda: send_near(jnp.minimum(j + SLOTS - DELAY, SLOTS - 1)))
        send_dx(j)
        for i, step in enumerate(steps[:SLOTS]):
            pl.when(j == i)(step)
        feed(j + SLOTS, 2 * SLOTS)
        forward(j)

    each(last)
    for step in steps[SLOTS:]:
        step()

    swapped = keys.at[:, :, pl.ds(0, TOK)]
    paired = keys.at[:, :, pl.ds(0, PAIR)]
    wait_bytes(swapped, send_sem.at[SWAP])
    wait_bytes(cot.at[:, pl.ds(0, TOK)], send_sem.at[COT])
    wait_bytes(pos.at[:, 0], send_sem.at[POS])
    pl.when(up)(lambda: wait_bytes(paired, send_sem.at[PAIRS]))
    pl.when(up & down)(lambda: wait_bytes(paired, send_sem.at[RELAY]))
    pl.when(down)(lambda: wait_bytes(from_near, send_sem.at[NEARG]))
    pl.when(down2)(lambda: wait_bytes(from_far, send_sem.at[FARG]))
    upward = jnp.where(up, level + 1, 0)
    downward = jnp.where(down, levels - level, 0)

    @pl.loop(0, upward + downward)
    def _(_i):
        wait_bytes(columns.at[0], pos_sem.at[4])

    half_copy().wait_send()
    for stage, (_, _, factor) in enumerate(stages):
        for offset in range(1, factor):
            sum_copy(stage, offset, digit_of(stage)).wait_send()
    for kind, (sent, target) in enumerate(((produced, next_ref), (dx, up_ref))):
        wait_bytes(sent, send_sem.at[OUT + kind])
        wait_bytes(target, out_recv.at[kind])


def place(produced_ref, grads_ref, total_ref, next_ref, up_ref, gain_ref, sem):
    pairs = ((produced_ref, next_ref), (grads_ref, up_ref), (total_ref, gain_ref))
    copies = [
        pltpu.make_async_copy(source, target, sem.at[i])
        for i, (source, target) in enumerate(pairs)
    ]
    for copy in copies:
        copy.start()
    for copy in copies:
        copy.wait()


def local(
    sizes,
    section_input,
    section_positions,
    saved_input,
    saved_positions,
    cotangent,
    norm_gains,
    output_gains,
    plan,
):
    stages = sum_stages(sizes)
    widest = max([factor for _, _, factor in stages] + [2])
    depth = max(len(stages), 1)
    levels = sizes["ctx"] // 2
    anywhere = pl.BlockSpec(memory_space=pl.ANY)
    in_vmem = pl.BlockSpec(memory_space=pltpu.VMEM)
    shapes = (
        jax.ShapeDtypeStruct((TOK, FEATURES), BF16),
        jax.ShapeDtypeStruct((TOK, FEATURES), BF16),
        jax.ShapeDtypeStruct((3 * HEADS, HEAD_DIM), F32),
    )
    results = pl.pallas_call(
        functools.partial(kernel, sizes),
        out_shape=shapes,
        in_specs=[anywhere] * 8,
        out_specs=(anywhere, anywhere, in_vmem),
        scratch_shapes=[
            pltpu.VMEM((2, SLOTS, SPAN, HEAD_DIM), BF16),
            pltpu.VMEM((SLOTS, PAIR, HEAD_DIM), BF16),
            pltpu.VMEM((2, 2, 1, TOK), jnp.int32),
            pltpu.VMEM((2, 2, FEATURES), F32),
            pltpu.VMEM((2, 1, FEATURES), F32),
            pltpu.SMEM((1, 2), jnp.int32),
            pltpu.VMEM((8, FEATURES), F32),
            pltpu.VMEM((2, SPAN, PAIR), F32),
            pltpu.VMEM((SLOTS, WINDOW, HEAD_DIM), BF16),
            pltpu.VMEM((SLOTS, PAIR, HEAD_DIM), F32),
            pltpu.VMEM((SLOTS, PAIR, HEAD_DIM), BF16),
            pltpu.VMEM((SLOTS, PAIR, HEAD_DIM), BF16),
            pltpu.VMEM((SLOTS, PAIR, HEAD_DIM), BF16),
            pltpu.VMEM((SLOTS, PAIR, HEAD_DIM), BF16),
            pltpu.VMEM((depth, widest, 3 * SLOTS, HEAD_DIM), F32),
            pltpu.VMEM((levels, 3 * SLOTS, HEAD_DIM), F32),
            pltpu.VMEM((2, 3 * SLOTS, HEAD_DIM), F32),
            pltpu.SemaphoreType.DMA((3,)),
            pltpu.SemaphoreType.DMA((5,)),
            pltpu.SemaphoreType.DMA((5,)),
            pltpu.SemaphoreType.DMA((2 * SLOTS,)),
            pltpu.SemaphoreType.DMA((SLOTS,)),
            pltpu.SemaphoreType.DMA((2 * SLOTS,)),
            pltpu.SemaphoreType.DMA((2 * SLOTS,)),
            pltpu.SemaphoreType.DMA((SLOTS,)),
            pltpu.SemaphoreType.DMA((SLOTS,)),
            pltpu.SemaphoreType.DMA((2,)),
            pltpu.SemaphoreType.DMA((9,)),
            pltpu.SemaphoreType.DMA((depth, widest - 1)),
            pltpu.SemaphoreType.DMA((depth, widest - 1)),
            pltpu.SemaphoreType.DMA((levels,)),
        ],
        compiler_params=pltpu.CompilerParams(
            collective_id=0, has_side_effects=True, vmem_limit_bytes=24 * 1024 * 1024
        ),
        cost_estimate=pl.CostEstimate(
            flops=9 * 2 * TOK * SPAN * FEATURES,
            bytes_accessed=5 * TOK * FEATURES * 2,
            transcendentals=2 * HEADS * TOK * SPAN,
        ),
    )(
        *(
            pltpu.with_memory_space_constraint(array, pltpu.MemorySpace.HBM)
            for array in (
                section_input[0, 0],
                section_positions[0],
                saved_input[0, 0],
                saved_positions[0],
                cotangent[0, 0],
                norm_gains[:, 0],
                output_gains,
                plan[0],
            )
        )
    )
    produced, grads, totals = pl.pallas_call(
        place,
        out_shape=shapes,
        in_specs=[anywhere] * 3,
        out_specs=(anywhere,) * 3,
        scratch_shapes=[pltpu.SemaphoreType.DMA((3,))],
        compiler_params=pltpu.CompilerParams(vmem_limit_bytes=1024 * 1024),
    )(*results)
    return (produced[None, None], grads[None, None], totals.reshape(1, 3, FEATURES))


def solution(mesh):
    placed = (
        P("dp", "pipe", "ctx", None),
        P("dp", "pipe", "ctx"),
        P("dp", "pipe", "ctx", None),
        P("dp", "pipe", "ctx"),
        P("dp", "pipe", "ctx", None),
        P(None, "pipe", None, None),
        P(None, "pipe", None),
        P("dp", "pipe", None),
    )
    return jax.shard_map(
        functools.partial(local, {axis: mesh.shape[axis] for axis in ("dp", "pipe", "ctx")}),
        mesh=mesh,
        in_specs=placed,
        out_specs=(
            P("dp", "pipe", "ctx", None),
            P("dp", "pipe", "ctx", None),
            P("pipe", None, None),
        ),
        check_vma=False,
    )
```

```python
import functools

import jax
import jax.numpy as jnp
from jax import lax
from jax.experimental import pallas as pl
from jax.experimental.pallas import tpu as pltpu
from jax.sharding import PartitionSpec as P

HEADS = 16
HEAD_DIM = 128
FEATURES = 2048
WINDOW = 512
TOK = 128
PAIR = 2 * TOK
SPAN = WINDOW + PAIR
SLOTS = HEADS // 2
OWN_AHEAD = 8
AHEAD = 3
PASS = 2
DELAY = 4
GATHER = 6
EPSILON = 1e-06
SCALE = HEAD_DIM**-0.5
LOG2E = 1.4426950408889634
MESH = pl.DeviceIdType.MESH
F32 = jnp.float32
BF16 = jnp.bfloat16
FAR, NEAR, OWN = 0, PAIR, 2 * PAIR


def sum_stages(sizes):
    stages = []
    left, stride = sizes["dp"], 1
    while left > 1:
        factor = next(f for f in range(2, left + 1) if left % f == 0)
        stages.append(("dp", stride, factor))
        left //= factor
        stride *= factor
    return stages


def dot(left, right, left_dim, right_dim):
    return lax.dot_general(
        left, right, (((left_dim,), (right_dim,)), ((), ())), preferred_element_type=F32
    )


def kernel(
    sizes,
    sec_ref,
    sec_pos,
    sav_ref,
    sav_pos,
    cot_ref,
    norm_ref,
    outg_ref,
    plan_ref,
    next_ref,
    up_ref,
    total_ref,
    keys,
    cot,
    pos,
    norm_in,
    outg_in,
    plan_in,
    gains,
    masks,
    grads,
    own,
    from_near,
    from_far,
    produced,
    dx,
    sums,
    columns,
    halves,
    load_sem,
    small_sem,
    pos_sem,
    swap_recv,
    cot_recv,
    pair_recv,
    relay_recv,
    near_recv,
    far_recv,
    out_recv,
    send_sem,
    sum_send,
    sum_recv,
    column_recv,
):
    n = sizes["ctx"]
    c = lax.axis_index("ctx")
    side = lax.rem(c, 2)
    partner = c + 1 - 2 * side
    pipe = lax.axis_index("pipe")
    after = lax.rem(pipe + 1, sizes["pipe"])
    before = lax.rem(pipe + sizes["pipe"] - 1, sizes["pipe"])
    up, down = c + 2 < n, c >= 2
    down2 = c >= 4
    level, levels = c // 2, n // 2
    direct = levels <= 4
    stages = sum_stages(sizes)
    SWAP, COT, POS, PAIRS, RELAY, NEARG, FARG, OUT = range(8)

    def part(first, which):
        return pl.ds(pl.multiple_of(first + which * TOK, TOK), TOK)

    def lanes_of(h):
        return pl.ds(pl.multiple_of(h * HEAD_DIM, HEAD_DIM), HEAD_DIM)

    def remote(source, target, send, recv, device):
        return pltpu.make_async_remote_copy(
            src_ref=source,
            dst_ref=target,
            send_sem=send,
            recv_sem=recv,
            device_id=device,
            device_id_type=MESH,
        )

    def wait_bytes(ref, sem):
        pltpu.make_async_copy(ref, ref, sem).wait()

    def load(which, j):
        source = (sav_ref, sec_ref, cot_ref)[which]
        mine = part(0, side) if which == 2 else part(OWN, side)
        target = cot.at[j, mine] if which == 2 else keys.at[which, j, mine]
        return pltpu.make_async_copy(
            source.at[:, lanes_of(side * SLOTS + j)], target, load_sem.at[which]
        )

    def swap_copy(t, j):
        mine = part(OWN, side)
        return remote(
            (sav_ref, sec_ref)[t].at[:, lanes_of((1 - side) * SLOTS + j)],
            keys.at[t, j, mine],
            send_sem.at[SWAP],
            swap_recv.at[t * SLOTS + j],
            {"ctx": partner},
        )

    def cot_copy(j):
        return remote(
            cot_ref.at[:, lanes_of((1 - side) * SLOTS + j)],
            cot.at[j, part(0, side)],
            send_sem.at[COT],
            cot_recv.at[j],
            {"ctx": partner},
        )

    def pos_copy(t):
        return remote(
            (sav_pos, sec_pos)[t],
            pos.at[t, side],
            send_sem.at[POS],
            pos_sem.at[1],
            {"ctx": partner},
        )

    def pair_copy(s, which):
        t, j = s // SLOTS, lax.rem(s, SLOTS)
        return remote(
            keys.at[t, j, part(OWN, which)],
            keys.at[t, j, part(NEAR, which)],
            send_sem.at[PAIRS],
            pair_recv.at[s],
            {"ctx": c + 2},
        )

    def relay_copy(s):
        t, j = s // SLOTS, lax.rem(s, SLOTS)
        return remote(
            keys.at[t, j, pl.ds(NEAR, PAIR)],
            keys.at[t, j, pl.ds(FAR, PAIR)],
            send_sem.at[RELAY],
            relay_recv.at[s],
            {"ctx": c + 2},
        )

    def near_copy(j):
        return remote(
            grads.at[j, pl.ds(NEAR, PAIR)],
            from_near.at[j],
            send_sem.at[NEARG],
            near_recv.at[j],
            {"ctx": c - 2},
        )

    def far_copy(j):
        return remote(
            grads.at[j, pl.ds(FAR, PAIR)],
            from_far.at[j],
            send_sem.at[FARG],
            far_recv.at[j],
            {"ctx": c - 2},
        )

    def out_copy(kind, j, which):
        device = {"pipe": (after, before)[kind]}
        if which == 1:
            device["ctx"] = partner
        rows = part(0, side if which == 0 else 1 - side)
        return remote(
            (produced, dx)[kind].at[j, rows],
            (next_ref, up_ref)[kind].at[:, lanes_of(side * SLOTS + j)],
            send_sem.at[OUT + kind],
            out_recv.at[kind],
            device,
        )

    def digit_of(stage):
        axis, stride, factor = stages[stage]
        return lax.rem(lax.axis_index(axis) // stride, factor)

    def sum_peer(stage, offset):
        axis, stride, factor = stages[stage]
        digit = digit_of(stage)
        return {axis: lax.axis_index(axis) + (lax.rem(digit + offset, factor) - digit) * stride}

    def sum_copy(stage, offset, sender):
        return remote(
            sums.at[stage, digit_of(stage)],
            sums.at[stage, sender],
            sum_send.at[stage, offset - 1],
            sum_recv.at[stage, offset - 1],
            sum_peer(stage, offset),
        )

    def half_copy():
        return remote(
            halves.at[side],
            halves.at[side],
            pos_sem.at[2],
            pos_sem.at[3],
            {"ctx": partner},
        )

    def start_sum(stage):
        for offset in range(1, stages[stage][2]):
            sum_copy(stage, offset, digit_of(stage)).start()

    def finish_sum(stage):
        factor = stages[stage][2]
        for offset in range(1, factor):
            sender = lax.rem(digit_of(stage) + factor - offset, factor)
            sum_copy(stage, offset, sender).wait_recv()
        total = sums[stage, 0]
        for digit in range(1, factor):
            total = total + sums[stage, digit]
        if stage + 1 < len(stages):
            sums[stage + 1, digit_of(stage + 1)] = total
            start_sum(stage + 1)
        else:
            start_column(total)

    def column_copy(which, step):
        return remote(
            columns.at[which],
            columns.at[which],
            pos_sem.at[4],
            column_recv.at[which],
            {"ctx": c + step},
        )

    def start_column(total):
        columns[level] = total
        for k in range(1, levels if direct else 2):
            pl.when(level + k < levels)(lambda: column_copy(level, 2 * k).start())
            pl.when(level >= k)(lambda: column_copy(level, -2 * k).start())

    def pass_column(k):
        below, above = level - k, level + k

        @pl.when(below >= 0)
        def _():
            wait_bytes(columns.at[0], column_recv.at[below])
            pl.when(up)(lambda: column_copy(below, 2).start())

        @pl.when(above < levels)
        def _():
            wait_bytes(columns.at[0], column_recv.at[above])
            pl.when(down)(lambda: column_copy(above, -2).start())

    def finish_column():
        if direct:
            for which in range(levels):
                pl.when(level != which)(
                    lambda: wait_bytes(columns.at[0], column_recv.at[which])
                )
        else:
            for k in range(1, levels):
                pass_column(k)
        total = columns[0]
        for which in range(1, levels):
            total = total + columns[which]
        finish_half(total)

    def finish_half(total):
        halves[side] = total * (1.0 / TOK)
        half_copy().start()

    def finish_total():
        half_copy().wait_recv()
        for which in range(2):
            for m in range(3):
                total_ref[pl.ds(m * HEADS + which * SLOTS, SLOTS), :] = halves[
                    which, pl.ds(m * SLOTS, SLOTS), :
                ]

    def each(action):
        @pl.loop(0, SLOTS)
        def _(j):
            action(j)

    barrier = pltpu.get_barrier_semaphore()

    def greet(device):
        pl.semaphore_signal(barrier, inc=1, device_id=device, device_id_type=MESH)

    greet({"ctx": partner})
    greet({"pipe": after})
    greet({"ctx": partner, "pipe": after})
    count = 3
    if sizes["pipe"] > 2:
        greet({"pipe": before})
        greet({"ctx": partner, "pipe": before})
        count += 2
    for condition, device in ((up, c + 2), (down, c - 2)):
        pl.when(condition)(lambda: greet({"ctx": device}))
        count = count + condition.astype(jnp.int32)
    for stage, (_, _, factor) in enumerate(stages):
        for offset in range(1, factor):
            greet(sum_peer(stage, offset))
            count += 1

    each(lambda j: load(0, j).start())
    small = (
        (norm_ref, norm_in),
        (outg_ref, outg_in),
        (plan_ref, plan_in),
        (sav_pos, pos.at[0, side]),
        (sec_pos, pos.at[1, side]),
    )
    for i, (source, target) in enumerate(small):
        pltpu.make_async_copy(source, target, small_sem.at[i]).start()
    each(lambda j: load(2, j).start())
    each(lambda j: load(1, j).start())
    wait_bytes(keys.at[0, :, pl.ds(0, TOK)], load_sem.at[0])
    pl.semaphore_wait(barrier, count)

    def pass_pair(s, which):
        pl.when(up)(lambda: pair_copy(s, which).start())

    def relay(s):
        @pl.when(down)
        def _():
            wait_bytes(keys.at[0, 0, pl.ds(NEAR, PAIR)], pair_recv.at[s])
            pl.when(up)(lambda: relay_copy(s).start())

    def wait_swap(s):
        wait_bytes(keys.at[0, 0, pl.ds(0, TOK)], swap_recv.at[s])

    for t in range(2):
        pos_copy(t).start()

    def first_swaps(j):
        swap_copy(0, j).start()
        pl.when(j < OWN_AHEAD)(lambda: pass_pair(j, side))
        cot_copy(j).start()

    each(first_swaps)
    each(lambda j: swap_copy(1, j).start())

    for i, (source, target) in enumerate(small):
        pltpu.make_async_copy(source, target, small_sem.at[i]).wait()
    for which in range(2):
        lap = plan_in[0, which]
        gains[pl.ds(3 * which, 2), :] = jnp.where(lap == 1, norm_in[1], norm_in[0])
        gains[pl.ds(3 * which + 2, 1), :] = jnp.where(lap == 1, outg_in[1], outg_in[0])
    for reach, first in ((2, NEAR), (4, FAR)):

        @pl.when(c < reach)
        def _():
            @pl.loop(0, SLOTS)
            def _(j):
                for t in range(2):
                    keys[t, j, pl.ds(first, PAIR)] = jnp.zeros((PAIR, HEAD_DIM), BF16)

    for s in range(AHEAD):
        wait_swap(s)
        pass_pair(s, 1 - side)

    wait_bytes(pos.at[:, 0], pos_sem.at[1])
    distance = (
        lax.broadcasted_iota(jnp.int32, (SPAN, TOK), 1)
        + WINDOW
        - lax.broadcasted_iota(jnp.int32, (SPAN, TOK), 0)
    )
    for t in range(2):
        for which in range(2):
            apart = distance + which * TOK
            allowed = (apart >= 0) & (apart < WINDOW) & (apart <= pos[t, which])
            masks[t, :, pl.ds(which * TOK, TOK)] = jnp.where(allowed, 1.0, 0.0).astype(F32)

    wait_bytes(cot.at[:, pl.ds(0, TOK)], load_sem.at[2])
    wait_bytes(keys.at[1, :, pl.ds(0, TOK)], load_sem.at[1])
    for s in range(PASS):
        relay(s)

    def normed(x):
        wide = x.astype(F32)
        inverse = lax.rsqrt(jnp.mean(wide * wide, axis=-1, keepdims=True) + EPSILON)
        return wide * inverse, inverse

    def weights(t, k, q, queries):
        w = jnp.exp2(dot(k, q, 1, 1) * (SCALE * LOG2E)) * masks[t, :, queries]
        return w, 1.0 / jnp.sum(w, axis=0, keepdims=True)

    sum_slot = digit_of(0) if stages else 0

    def backward(j):
        wide = lanes_of(side * SLOTS + j)
        a, b, g = (gains[pl.ds(3 + m, 1), wide] for m in range(3))
        x = keys[0, j]
        n_all, inverse = normed(x)
        k = (n_all * b).astype(BF16)
        q = (n_all[WINDOW:] * a).astype(BF16)
        w, sum_inverse = weights(0, k, q, pl.ds(0, PAIR))
        prob = w * sum_inverse
        p = prob.astype(BF16)
        ct = cot[j].astype(F32)
        d_mix = (ct * g).astype(BF16)
        d_prob = dot(x, d_mix, 1, 1)
        delta = jnp.sum(prob * d_prob, axis=0, keepdims=True)
        d_score = (prob * (d_prob - delta)).astype(BF16)
        d_k = dot(d_score, q, 1, 0)
        d_q = dot(k, d_score, 0, 0).T
        mixed = dot(p, cot[j], 1, 0)
        d_value = mixed * g
        n_own = n_all[WINDOW:]
        d_n = d_k * (b * SCALE)
        d_n_own = d_n[WINDOW:] + d_q * (a * SCALE)

        def through_norm(d, value, scale):
            return scale * (d - value * jnp.mean(d * value, axis=-1, keepdims=True))

        grads[j] = (
            d_value[:WINDOW] + through_norm(d_n[:WINDOW], n_all[:WINDOW], inverse[:WINDOW])
        ).astype(BF16)
        own[j] = d_value[WINDOW:] + through_norm(d_n_own, n_own, inverse[WINDOW:]) + ct
        parts = (
            jnp.sum(d_q * n_own, axis=0, keepdims=True) * SCALE,
            jnp.sum(d_k * n_all, axis=0, keepdims=True) * SCALE,
            jnp.sum(mixed * x, axis=0, keepdims=True),
        )
        for m in range(3):
            sums[0, sum_slot, pl.ds(m * SLOTS + j, 1), :] = parts[m]

    def forward(j):
        wide = lanes_of(side * SLOTS + j)
        a, b, g = (gains[pl.ds(m, 1), wide] for m in range(3))
        x = keys[1, j]
        k = (normed(x)[0] * b).astype(BF16)
        for which in (1, 0):
            rows = side if which == 0 else 1 - side
            mine = keys[1, j, part(OWN, rows)]
            q = (normed(mine)[0] * a).astype(BF16)
            w, inverse = weights(1, k, q, part(0, rows))
            mix = (dot(x, w.astype(BF16), 0, 0) * inverse).T
            produced[j, part(0, rows)] = (mine.astype(F32) + g * mix).astype(BF16)
            out_copy(0, j, which).start()

    def feed(s, total):
        @pl.when(s + AHEAD < total)
        def _():
            wait_swap(s + AHEAD)
            pass_pair(s + AHEAD, 1 - side)

        pl.when(s + OWN_AHEAD < total)(lambda: pass_pair(s + OWN_AHEAD, side))

        pl.when(s + PASS < total)(lambda: relay(s + PASS))

    def await_far(s):
        pl.when(down2)(lambda: wait_bytes(keys.at[0, 0, pl.ds(FAR, PAIR)], relay_recv.at[s]))

    def send_near(j):
        @pl.when(up & down)
        def _():
            far_copy(j).wait_recv()
            near = grads[j, pl.ds(NEAR, PAIR)].astype(F32) + from_far[j].astype(F32)
            grads[j, pl.ds(NEAR, PAIR)] = near.astype(BF16)
            near_copy(j).start()

    def first(j):
        feed(j, 2 * SLOTS)
        await_far(j)
        wait_bytes(cot.at[0, pl.ds(0, TOK)], cot_recv.at[j])
        backward(j)
        pl.when(down2)(lambda: far_copy(j).start())
        pl.when(down & jnp.logical_not(up))(lambda: near_copy(j).start())
        pl.when(j >= DELAY)(lambda: send_near(jnp.maximum(j - DELAY, 0)))

    each(first)
    if stages:
        start_sum(0)
    else:
        start_column(sums[0, 0])

    def send_dx(j):
        @pl.when(up)
        def _():
            near_copy(j).wait_recv()
            own[j] = own[j] + from_near[j].astype(F32)

        dx[j] = own[j].astype(BF16)
        for which in range(2):
            out_copy(1, j, which).start()

    def last(j):
        feed(j + SLOTS, 2 * SLOTS)
        pl.when(j < DELAY)(lambda: send_near(jnp.minimum(j + SLOTS - DELAY, SLOTS - 1)))
        send_dx(j)
        for stage in range(len(stages)):
            pl.when(j == min(stage + 1, GATHER - 1))(lambda: finish_sum(stage))
        if direct:
            pl.when(j == GATHER)(finish_column)
        await_far(j + SLOTS)
        forward(j)

    each(last)
    if not direct:
        finish_column()
    finish_total()

    swapped = keys.at[:, :, pl.ds(0, TOK)]
    paired = keys.at[:, :, pl.ds(0, PAIR)]
    wait_bytes(swapped, send_sem.at[SWAP])
    wait_bytes(cot.at[:, pl.ds(0, TOK)], send_sem.at[COT])
    wait_bytes(pos.at[:, 0], send_sem.at[POS])
    pl.when(up)(lambda: wait_bytes(paired, send_sem.at[PAIRS]))
    pl.when(up & down)(lambda: wait_bytes(paired, send_sem.at[RELAY]))
    pl.when(down)(lambda: wait_bytes(from_near, send_sem.at[NEARG]))
    pl.when(down2)(lambda: wait_bytes(from_far, send_sem.at[FARG]))
    if direct:
        wait_bytes(columns.at[pl.ds(0, levels - 1)], pos_sem.at[4])
    else:
        upward = jnp.where(up, level + 1, 0)
        downward = jnp.where(down, levels - level, 0)

        @pl.loop(0, upward + downward)
        def _(_):
            wait_bytes(columns.at[0], pos_sem.at[4])

    half_copy().wait_send()
    for stage, (_, _, factor) in enumerate(stages):
        for offset in range(1, factor):
            sum_copy(stage, offset, digit_of(stage)).wait_send()
    for kind, (sent, target) in enumerate(((produced, next_ref), (dx, up_ref))):
        wait_bytes(sent, send_sem.at[OUT + kind])
        wait_bytes(target, out_recv.at[kind])


def place(produced_ref, grads_ref, total_ref, next_ref, up_ref, gain_ref, sem):
    pairs = ((produced_ref, next_ref), (grads_ref, up_ref), (total_ref, gain_ref))
    copies = [
        pltpu.make_async_copy(source, target, sem.at[i])
        for i, (source, target) in enumerate(pairs)
    ]
    for copy in copies:
        copy.start()
    for copy in copies:
        copy.wait()


def local(
    sizes,
    section_input,
    section_positions,
    saved_input,
    saved_positions,
    cotangent,
    norm_gains,
    output_gains,
    plan,
):
    stages = sum_stages(sizes)
    widest = max([factor for _, _, factor in stages] + [2])
    depth = max(len(stages), 1)
    levels = sizes["ctx"] // 2
    anywhere = pl.BlockSpec(memory_space=pl.ANY)
    in_vmem = pl.BlockSpec(memory_space=pltpu.VMEM)
    shapes = (
        jax.ShapeDtypeStruct((TOK, FEATURES), BF16),
        jax.ShapeDtypeStruct((TOK, FEATURES), BF16),
        jax.ShapeDtypeStruct((3 * HEADS, HEAD_DIM), F32),
    )
    results = pl.pallas_call(
        functools.partial(kernel, sizes),
        out_shape=shapes,
        in_specs=[anywhere] * 8,
        out_specs=(anywhere, anywhere, in_vmem),
        scratch_shapes=[
            pltpu.VMEM((2, SLOTS, SPAN, HEAD_DIM), BF16),
            pltpu.VMEM((SLOTS, PAIR, HEAD_DIM), BF16),
            pltpu.VMEM((2, 2, 1, TOK), jnp.int32),
            pltpu.VMEM((2, 2, FEATURES), F32),
            pltpu.VMEM((2, 1, FEATURES), F32),
            pltpu.SMEM((1, 2), jnp.int32),
            pltpu.VMEM((8, FEATURES), F32),
            pltpu.VMEM((2, SPAN, PAIR), F32),
            pltpu.VMEM((SLOTS, WINDOW, HEAD_DIM), BF16),
            pltpu.VMEM((SLOTS, PAIR, HEAD_DIM), F32),
            pltpu.VMEM((SLOTS, PAIR, HEAD_DIM), BF16),
            pltpu.VMEM((SLOTS, PAIR, HEAD_DIM), BF16),
            pltpu.VMEM((SLOTS, PAIR, HEAD_DIM), BF16),
            pltpu.VMEM((SLOTS, PAIR, HEAD_DIM), BF16),
            pltpu.VMEM((depth, widest, 3 * SLOTS, HEAD_DIM), F32),
            pltpu.VMEM((levels, 3 * SLOTS, HEAD_DIM), F32),
            pltpu.VMEM((2, 3 * SLOTS, HEAD_DIM), F32),
            pltpu.SemaphoreType.DMA((3,)),
            pltpu.SemaphoreType.DMA((5,)),
            pltpu.SemaphoreType.DMA((5,)),
            pltpu.SemaphoreType.DMA((2 * SLOTS,)),
            pltpu.SemaphoreType.DMA((SLOTS,)),
            pltpu.SemaphoreType.DMA((2 * SLOTS,)),
            pltpu.SemaphoreType.DMA((2 * SLOTS,)),
            pltpu.SemaphoreType.DMA((SLOTS,)),
            pltpu.SemaphoreType.DMA((SLOTS,)),
            pltpu.SemaphoreType.DMA((2,)),
            pltpu.SemaphoreType.DMA((9,)),
            pltpu.SemaphoreType.DMA((depth, widest - 1)),
            pltpu.SemaphoreType.DMA((depth, widest - 1)),
            pltpu.SemaphoreType.DMA((levels,)),
        ],
        compiler_params=pltpu.CompilerParams(
            collective_id=0, has_side_effects=True, vmem_limit_bytes=24 * 1024 * 1024
        ),
        cost_estimate=pl.CostEstimate(
            flops=9 * 2 * TOK * SPAN * FEATURES,
            bytes_accessed=5 * TOK * FEATURES * 2,
            transcendentals=2 * HEADS * TOK * SPAN,
        ),
    )(
        *(
            pltpu.with_memory_space_constraint(array, pltpu.MemorySpace.HBM)
            for array in (
                section_input[0, 0],
                section_positions[0],
                saved_input[0, 0],
                saved_positions[0],
                cotangent[0, 0],
                norm_gains[:, 0],
                output_gains,
                plan[0],
            )
        )
    )
    produced, grads, totals = pl.pallas_call(
        place,
        out_shape=shapes,
        in_specs=[anywhere] * 3,
        out_specs=(anywhere,) * 3,
        scratch_shapes=[pltpu.SemaphoreType.DMA((3,))],
        compiler_params=pltpu.CompilerParams(vmem_limit_bytes=1024 * 1024),
    )(*results)
    return (produced[None, None], grads[None, None], totals.reshape(1, 3, FEATURES))


def solution(mesh):
    placed = (
        P("dp", "pipe", "ctx", None),
        P("dp", "pipe", "ctx"),
        P("dp", "pipe", "ctx", None),
        P("dp", "pipe", "ctx"),
        P("dp", "pipe", "ctx", None),
        P(None, "pipe", None, None),
        P(None, "pipe", None),
        P("dp", "pipe", None),
    )
    return jax.shard_map(
        functools.partial(local, {axis: mesh.shape[axis] for axis in ("dp", "pipe", "ctx")}),
        mesh=mesh,
        in_specs=placed,
        out_specs=(
            P("dp", "pipe", "ctx", None),
            P("dp", "pipe", "ctx", None),
            P("pipe", None, None),
        ),
        check_vma=False,
    )
```

```python
import functools

import jax
import jax.numpy as jnp
from jax import lax
from jax.experimental import pallas as pl
from jax.experimental.pallas import tpu as pltpu
from jax.sharding import PartitionSpec as P

HEADS = 16
HEAD_DIM = 128
FEATURES = 2048
WINDOW = 512
TOK = 128
PAIR = 2 * TOK
SPAN = WINDOW + PAIR
SLOTS = HEADS // 2
OWN_AHEAD = 8
AHEAD = 4
PASS = 2
DELAY = 4
GATHER = 6
EPSILON = 1e-06
SCALE = HEAD_DIM**-0.5
LOG2E = 1.4426950408889634
MESH = pl.DeviceIdType.MESH
F32 = jnp.float32
BF16 = jnp.bfloat16
FAR, NEAR, OWN = 0, PAIR, 2 * PAIR


def dot(left, right, left_dim, right_dim):
    return lax.dot_general(
        left, right, (((left_dim,), (right_dim,)), ((), ())), preferred_element_type=F32
    )


def kernel(
    sizes,
    sec_ref,
    sec_pos,
    sav_ref,
    sav_pos,
    cot_ref,
    norm_ref,
    outg_ref,
    plan_ref,
    next_ref,
    up_ref,
    total_ref,
    keys,
    cot,
    pos,
    norm_in,
    outg_in,
    plan_in,
    gains,
    masks,
    grads,
    own,
    from_near,
    from_far,
    produced,
    dx,
    sums,
    parts,
    columns,
    shares,
    load_sem,
    small_sem,
    pos_sem,
    swap_recv,
    cot_recv,
    pair_recv,
    relay_recv,
    near_recv,
    far_recv,
    out_recv,
    send_sem,
    gain_sem,
):
    n = sizes["ctx"]
    c = lax.axis_index("ctx")
    side = lax.rem(c, 2)
    partner = c + 1 - 2 * side
    pipe = lax.axis_index("pipe")
    after = lax.rem(pipe + 1, sizes["pipe"])
    before = lax.rem(pipe + sizes["pipe"] - 1, sizes["pipe"])
    up, down = c + 2 < n, c >= 2
    down2 = c >= 4
    level, levels = c // 2, n // 2
    direct = levels <= 4
    replica, replicas = lax.axis_index("dp"), sizes["dp"]
    per = SLOTS // replicas
    SWAP, COT, POS, PAIRS, RELAY, NEARG, FARG, OUT = range(8)

    def part(first, which):
        return pl.ds(pl.multiple_of(first + which * TOK, TOK), TOK)

    def lanes_of(h):
        return pl.ds(pl.multiple_of(h * HEAD_DIM, HEAD_DIM), HEAD_DIM)

    def remote(source, target, send, recv, device):
        return pltpu.make_async_remote_copy(
            src_ref=source,
            dst_ref=target,
            send_sem=send,
            recv_sem=recv,
            device_id=device,
            device_id_type=MESH,
        )

    def wait_bytes(ref, sem):
        pltpu.make_async_copy(ref, ref, sem).wait()

    def load(which, j):
        source = (sav_ref, sec_ref, cot_ref)[which]
        mine = part(0, side) if which == 2 else part(OWN, side)
        target = cot.at[j, mine] if which == 2 else keys.at[which, j, mine]
        return pltpu.make_async_copy(
            source.at[:, lanes_of(side * SLOTS + j)], target, load_sem.at[which]
        )

    def swap_copy(t, j):
        mine = part(OWN, side)
        return remote(
            (sav_ref, sec_ref)[t].at[:, lanes_of((1 - side) * SLOTS + j)],
            keys.at[t, j, mine],
            send_sem.at[SWAP],
            swap_recv.at[t * SLOTS + j],
            {"ctx": partner},
        )

    def cot_copy(j):
        return remote(
            cot_ref.at[:, lanes_of((1 - side) * SLOTS + j)],
            cot.at[j, part(0, side)],
            send_sem.at[COT],
            cot_recv.at[j],
            {"ctx": partner},
        )

    def pos_copy(t):
        return remote(
            (sav_pos, sec_pos)[t],
            pos.at[t, side],
            send_sem.at[POS],
            pos_sem.at[1],
            {"ctx": partner},
        )

    def pair_copy(s, which):
        t, j = s // SLOTS, lax.rem(s, SLOTS)
        return remote(
            keys.at[t, j, part(OWN, which)],
            keys.at[t, j, part(NEAR, which)],
            send_sem.at[PAIRS],
            pair_recv.at[s],
            {"ctx": c + 2},
        )

    def relay_copy(s):
        t, j = s // SLOTS, lax.rem(s, SLOTS)
        return remote(
            keys.at[t, j, pl.ds(NEAR, PAIR)],
            keys.at[t, j, pl.ds(FAR, PAIR)],
            send_sem.at[RELAY],
            relay_recv.at[s],
            {"ctx": c + 2},
        )

    def near_copy(j):
        return remote(
            grads.at[j, pl.ds(NEAR, PAIR)],
            from_near.at[j],
            send_sem.at[NEARG],
            near_recv.at[j],
            {"ctx": c - 2},
        )

    def far_copy(j):
        return remote(
            grads.at[j, pl.ds(FAR, PAIR)],
            from_far.at[j],
            send_sem.at[FARG],
            far_recv.at[j],
            {"ctx": c - 2},
        )

    def out_copy(kind, j, which):
        device = {"pipe": (after, before)[kind]}
        if which == 1:
            device["ctx"] = partner
        rows = part(0, side if which == 0 else 1 - side)
        return remote(
            (produced, dx)[kind].at[j, rows],
            (next_ref, up_ref)[kind].at[:, lanes_of(side * SLOTS + j)],
            send_sem.at[OUT + kind],
            out_recv.at[kind],
            device,
        )

    def gain_copy(source, target, kind, device):
        return remote(source, target, gain_sem.at[kind], gain_sem.at[kind + 1], device)

    def start_sum():
        parts[replica] = sums[replica]
        for k in range(1, replicas):
            peer = lax.rem(replica + k, replicas)
            gain_copy(sums.at[peer], parts.at[replica], 0, {"dp": peer}).start()

    def column_copy():
        if direct:
            return gain_copy(columns.at[level], columns.at[level], 2, {"ctx": side})
        return gain_copy(columns.at[0], columns.at[1], 2, {"ctx": c - 2})

    def start_column():
        if replicas > 1:
            wait_bytes(parts.at[pl.ds(0, replicas - 1)], gain_sem.at[1])
        total = parts[0]
        for which in range(1, replicas):
            total = total + parts[which]
        columns[level if direct else 0] = total
        if direct:
            pl.when(level > 0)(lambda: column_copy().start())

    def spread(k):
        gain_copy(shares.at[side * replicas + replica], shares.at[side * replicas + replica], 4, {"ctx": c + 2 * k}).start()

    def top_column():
        wait_bytes(columns.at[pl.ds(0, levels - 1)], gain_sem.at[3])
        total = columns[0]
        for which in range(1, levels):
            total = total + columns[which]
        shares[side * replicas + replica] = total * (1.0 / TOK)
        for k in range(1, levels):
            spread(k)

    def chain_column():
        @pl.when(up)
        def _():
            wait_bytes(columns.at[0], gain_sem.at[3])
            columns[0] = columns[0] + columns[1]

        pl.when(down)(lambda: column_copy().start())

        @pl.when(level == 0)
        def _():
            shares[side * replicas + replica] = columns[0] * (1.0 / TOK)

    def start_share():
        pl.when(level > 0)(lambda: wait_bytes(columns.at[0], gain_sem.at[5]))
        if not direct:
            pl.when(up)(lambda: spread(1))
        for k in range(replicas):
            peer = lax.rem(replica + k, replicas)
            for which in ([partner] if k == 0 else [c, partner]):
                gain_copy(
                    shares.at[side * replicas + replica],
                    shares.at[side * replicas + replica],
                    6,
                    {"ctx": which, "dp": peer},
                ).start()

    def wait_shares(kind):
        wait_bytes(shares.at[pl.ds(0, 2 * replicas - 1)], gain_sem.at[kind])

    def finish_total():
        wait_shares(7)
        for which in range(2):
            for chunk in range(replicas):
                for m in range(3):
                    first = m * HEADS + which * SLOTS + chunk * per
                    total_ref[pl.ds(first, per), :] = shares[which * replicas + chunk, pl.ds(m * per, per), :]

    def each(action):
        @pl.loop(0, SLOTS)
        def _(j):
            action(j)

    barrier = pltpu.get_barrier_semaphore()

    def greet(device):
        pl.semaphore_signal(barrier, inc=1, device_id=device, device_id_type=MESH)

    greet({"ctx": partner})
    greet({"pipe": after})
    greet({"ctx": partner, "pipe": after})
    count = 3
    if sizes["pipe"] > 2:
        greet({"pipe": before})
        greet({"ctx": partner, "pipe": before})
        count += 2
    for condition, device in ((up, c + 2), (down, c - 2)):
        pl.when(condition)(lambda: greet({"ctx": device}))
        count = count + condition.astype(jnp.int32)
    for k in range(1, replicas):
        greet({"dp": lax.rem(replica + k, replicas)})
        count += 1

    each(lambda j: load(0, j).start())
    small = (
        (norm_ref, norm_in),
        (outg_ref, outg_in),
        (plan_ref, plan_in),
        (sav_pos, pos.at[0, side]),
        (sec_pos, pos.at[1, side]),
    )
    for i, (source, target) in enumerate(small):
        pltpu.make_async_copy(source, target, small_sem.at[i]).start()
    each(lambda j: load(2, j).start())
    each(lambda j: load(1, j).start())
    wait_bytes(keys.at[0, :, pl.ds(0, TOK)], load_sem.at[0])
    pl.semaphore_wait(barrier, count)

    def pass_pair(s, which):
        pl.when(up)(lambda: pair_copy(s, which).start())

    def relay(s):
        @pl.when(down)
        def _():
            wait_bytes(keys.at[0, 0, pl.ds(NEAR, PAIR)], pair_recv.at[s])
            pl.when(up)(lambda: relay_copy(s).start())

    def wait_swap(s):
        wait_bytes(keys.at[0, 0, pl.ds(0, TOK)], swap_recv.at[s])

    for t in range(2):
        pos_copy(t).start()

    def first_swaps(j):
        swap_copy(0, j).start()
        pl.when(j < OWN_AHEAD)(lambda: pass_pair(j, side))
        cot_copy(j).start()

    each(first_swaps)
    each(lambda j: swap_copy(1, j).start())

    for i, (source, target) in enumerate(small):
        pltpu.make_async_copy(source, target, small_sem.at[i]).wait()
    for which in range(2):
        lap = plan_in[0, which]
        gains[pl.ds(3 * which, 2), :] = jnp.where(lap == 1, norm_in[1], norm_in[0])
        gains[pl.ds(3 * which + 2, 1), :] = jnp.where(lap == 1, outg_in[1], outg_in[0])
    for reach, first in ((2, NEAR), (4, FAR)):

        @pl.when(c < reach)
        def _():
            @pl.loop(0, SLOTS)
            def _(j):
                for t in range(2):
                    keys[t, j, pl.ds(first, PAIR)] = jnp.zeros((PAIR, HEAD_DIM), BF16)

    for s in range(AHEAD):
        wait_swap(s)
        pass_pair(s, 1 - side)

    wait_bytes(pos.at[:, 0], pos_sem.at[1])
    distance = (
        lax.broadcasted_iota(jnp.int32, (SPAN, TOK), 1)
        + WINDOW
        - lax.broadcasted_iota(jnp.int32, (SPAN, TOK), 0)
    )
    for t in range(2):
        for which in range(2):
            apart = distance + which * TOK
            allowed = (apart >= 0) & (apart < WINDOW) & (apart <= pos[t, which])
            masks[t, :, pl.ds(which * TOK, TOK)] = jnp.where(allowed, 1.0, 0.0).astype(F32)

    wait_bytes(cot.at[:, pl.ds(0, TOK)], load_sem.at[2])
    wait_bytes(keys.at[1, :, pl.ds(0, TOK)], load_sem.at[1])
    for s in range(PASS):
        relay(s)

    def normed(x):
        wide = x.astype(F32)
        inverse = lax.rsqrt(jnp.mean(wide * wide, axis=-1, keepdims=True) + EPSILON)
        return wide * inverse, inverse

    def weights(t, k, q, queries):
        w = jnp.exp2(dot(k, q, 1, 1) * (SCALE * LOG2E)) * masks[t, :, queries]
        return w, 1.0 / jnp.sum(w, axis=0, keepdims=True)

    def backward(j):
        wide = lanes_of(side * SLOTS + j)
        a, b, g = (gains[pl.ds(3 + m, 1), wide] for m in range(3))
        x = keys[0, j]
        n_all, inverse = normed(x)
        k = (n_all * b).astype(BF16)
        q = (n_all[WINDOW:] * a).astype(BF16)
        w, sum_inverse = weights(0, k, q, pl.ds(0, PAIR))
        prob = w * sum_inverse
        p = prob.astype(BF16)
        ct = cot[j].astype(F32)
        d_mix = (ct * g).astype(BF16)
        d_prob = dot(x, d_mix, 1, 1)
        delta = jnp.sum(prob * d_prob, axis=0, keepdims=True)
        d_score = (prob * (d_prob - delta)).astype(BF16)
        d_k = dot(d_score, q, 1, 0)
        d_q = dot(k, d_score, 0, 0).T
        mixed = dot(p, cot[j], 1, 0)
        d_value = mixed * g
        n_own = n_all[WINDOW:]
        d_n = d_k * (b * SCALE)
        d_n_own = d_n[WINDOW:] + d_q * (a * SCALE)

        def through_norm(d, value, scale):
            return scale * (d - value * jnp.mean(d * value, axis=-1, keepdims=True))

        grads[j] = (
            d_value[:WINDOW] + through_norm(d_n[:WINDOW], n_all[:WINDOW], inverse[:WINDOW])
        ).astype(BF16)
        own[j] = d_value[WINDOW:] + through_norm(d_n_own, n_own, inverse[WINDOW:]) + ct
        gained = (
            jnp.sum(d_q * n_own, axis=0, keepdims=True) * SCALE,
            jnp.sum(d_k * n_all, axis=0, keepdims=True) * SCALE,
            jnp.sum(mixed * x, axis=0, keepdims=True),
        )
        for m in range(3):
            sums[j // per, pl.ds(m * per + lax.rem(j, per), 1), :] = gained[m]

    def forward(j):
        wide = lanes_of(side * SLOTS + j)
        a, b, g = (gains[pl.ds(m, 1), wide] for m in range(3))

        def attend(first, length, queries):
            x = keys[1, j, pl.ds(first, length)]
            k = (normed(x)[0] * b).astype(BF16)
            found = []
            for q, rows in queries:
                scores = dot(k, q, 1, 1) * (SCALE * LOG2E)
                w = jnp.exp2(scores) * masks[1, pl.ds(first, length), part(0, rows)]
                found.append((jnp.sum(w, axis=0, keepdims=True), dot(x, w.astype(BF16), 0, 0)))
            return found

        queries = []
        for rows in (1 - side, side):
            mine = keys[1, j, part(OWN, rows)]
            queries.append(((normed(mine)[0] * a).astype(BF16), rows))
        close = attend(NEAR, SPAN - NEAR, queries)
        await_far(j + SLOTS)
        distant = attend(FAR, NEAR, queries)
        for which, (_, rows) in enumerate(queries):
            (sum_near, mix_near), (sum_far, mix_far) = close[which], distant[which]
            mix = ((mix_near + mix_far) * (1.0 / (sum_near + sum_far))).T
            mine = keys[1, j, part(OWN, rows)].astype(F32)
            produced[j, part(0, rows)] = (mine + g * mix).astype(BF16)
            out_copy(0, j, 1 - which).start()

    def feed(s, total):
        @pl.when(s + AHEAD < total)
        def _():
            wait_swap(s + AHEAD)
            pass_pair(s + AHEAD, 1 - side)

        pl.when(s + OWN_AHEAD < total)(lambda: pass_pair(s + OWN_AHEAD, side))

        pl.when(s + PASS < total)(lambda: relay(s + PASS))

    def await_far(s):
        pl.when(down2)(lambda: wait_bytes(keys.at[0, 0, pl.ds(FAR, PAIR)], relay_recv.at[s]))

    def send_near(j):
        @pl.when(up & down)
        def _():
            far_copy(j).wait_recv()
            near = grads[j, pl.ds(NEAR, PAIR)].astype(F32) + from_far[j].astype(F32)
            grads[j, pl.ds(NEAR, PAIR)] = near.astype(BF16)
            near_copy(j).start()

    def first(j):
        feed(j, 2 * SLOTS)
        await_far(j)
        wait_bytes(cot.at[0, pl.ds(0, TOK)], cot_recv.at[j])
        backward(j)
        pl.when(down2)(lambda: far_copy(j).start())
        pl.when(down & jnp.logical_not(up))(lambda: near_copy(j).start())
        pl.when(j >= DELAY)(lambda: send_near(jnp.maximum(j - DELAY, 0)))

    each(first)
    start_sum()

    def send_dx(j):
        @pl.when(up)
        def _():
            near_copy(j).wait_recv()
            own[j] = own[j] + from_near[j].astype(F32)

        dx[j] = own[j].astype(BF16)
        for which in range(2):
            out_copy(1, j, which).start()

    def last(j):
        feed(j + SLOTS, 2 * SLOTS)
        pl.when(j < DELAY)(lambda: send_near(jnp.minimum(j + SLOTS - DELAY, SLOTS - 1)))
        send_dx(j)
        pl.when(j == 1)(start_column)
        if direct:
            pl.when((j == GATHER) & (level == 0))(top_column)
            pl.when(j == GATHER + 1)(start_share)
        forward(j)

    each(last)
    if not direct:
        chain_column()
        start_share()
    finish_total()

    swapped = keys.at[:, :, pl.ds(0, TOK)]
    paired = keys.at[:, :, pl.ds(0, PAIR)]
    wait_bytes(swapped, send_sem.at[SWAP])
    wait_bytes(cot.at[:, pl.ds(0, TOK)], send_sem.at[COT])
    wait_bytes(pos.at[:, 0], send_sem.at[POS])
    pl.when(up)(lambda: wait_bytes(paired, send_sem.at[PAIRS]))
    pl.when(up & down)(lambda: wait_bytes(paired, send_sem.at[RELAY]))
    pl.when(down)(lambda: wait_bytes(from_near, send_sem.at[NEARG]))
    pl.when(down2)(lambda: wait_bytes(from_far, send_sem.at[FARG]))
    if replicas > 1:
        wait_bytes(sums.at[pl.ds(0, replicas - 1)], gain_sem.at[0])
    pl.when(level > 0)(lambda: wait_bytes(columns.at[0], gain_sem.at[2]))
    if direct:
        pl.when(level == 0)(lambda: wait_bytes(columns.at[pl.ds(0, levels - 1)], gain_sem.at[4]))
    else:
        pl.when(up)(lambda: wait_bytes(columns.at[0], gain_sem.at[4]))
    wait_shares(6)
    for kind, (sent, target) in enumerate(((produced, next_ref), (dx, up_ref))):
        wait_bytes(sent, send_sem.at[OUT + kind])
        wait_bytes(target, out_recv.at[kind])


def place(produced_ref, grads_ref, total_ref, next_ref, up_ref, gain_ref, sem):
    pairs = ((produced_ref, next_ref), (grads_ref, up_ref), (total_ref, gain_ref))
    copies = [
        pltpu.make_async_copy(source, target, sem.at[i])
        for i, (source, target) in enumerate(pairs)
    ]
    for copy in copies:
        copy.start()
    for copy in copies:
        copy.wait()


def local(
    sizes,
    section_input,
    section_positions,
    saved_input,
    saved_positions,
    cotangent,
    norm_gains,
    output_gains,
    plan,
):
    replicas, levels = sizes["dp"], sizes["ctx"] // 2
    part_shape = (3 * SLOTS // replicas, HEAD_DIM)
    anywhere = pl.BlockSpec(memory_space=pl.ANY)
    in_vmem = pl.BlockSpec(memory_space=pltpu.VMEM)
    shapes = (
        jax.ShapeDtypeStruct((TOK, FEATURES), BF16),
        jax.ShapeDtypeStruct((TOK, FEATURES), BF16),
        jax.ShapeDtypeStruct((3 * HEADS, HEAD_DIM), F32),
    )
    results = pl.pallas_call(
        functools.partial(kernel, sizes),
        out_shape=shapes,
        in_specs=[anywhere] * 8,
        out_specs=(anywhere, anywhere, in_vmem),
        scratch_shapes=[
            pltpu.VMEM((2, SLOTS, SPAN, HEAD_DIM), BF16),
            pltpu.VMEM((SLOTS, PAIR, HEAD_DIM), BF16),
            pltpu.VMEM((2, 2, 1, TOK), jnp.int32),
            pltpu.VMEM((2, 2, FEATURES), F32),
            pltpu.VMEM((2, 1, FEATURES), F32),
            pltpu.SMEM((1, 2), jnp.int32),
            pltpu.VMEM((8, FEATURES), F32),
            pltpu.VMEM((2, SPAN, PAIR), F32),
            pltpu.VMEM((SLOTS, WINDOW, HEAD_DIM), BF16),
            pltpu.VMEM((SLOTS, PAIR, HEAD_DIM), F32),
            pltpu.VMEM((SLOTS, PAIR, HEAD_DIM), BF16),
            pltpu.VMEM((SLOTS, PAIR, HEAD_DIM), BF16),
            pltpu.VMEM((SLOTS, PAIR, HEAD_DIM), BF16),
            pltpu.VMEM((SLOTS, PAIR, HEAD_DIM), BF16),
            pltpu.VMEM((replicas, *part_shape), F32),
            pltpu.VMEM((replicas, *part_shape), F32),
            pltpu.VMEM((levels, *part_shape), F32),
            pltpu.VMEM((2 * replicas, *part_shape), F32),
            pltpu.SemaphoreType.DMA((3,)),
            pltpu.SemaphoreType.DMA((5,)),
            pltpu.SemaphoreType.DMA((2,)),
            pltpu.SemaphoreType.DMA((2 * SLOTS,)),
            pltpu.SemaphoreType.DMA((SLOTS,)),
            pltpu.SemaphoreType.DMA((2 * SLOTS,)),
            pltpu.SemaphoreType.DMA((2 * SLOTS,)),
            pltpu.SemaphoreType.DMA((SLOTS,)),
            pltpu.SemaphoreType.DMA((SLOTS,)),
            pltpu.SemaphoreType.DMA((2,)),
            pltpu.SemaphoreType.DMA((9,)),
            pltpu.SemaphoreType.DMA((8,)),
        ],
        compiler_params=pltpu.CompilerParams(
            collective_id=0, has_side_effects=True, vmem_limit_bytes=24 * 1024 * 1024
        ),
        cost_estimate=pl.CostEstimate(
            flops=9 * 2 * TOK * SPAN * FEATURES,
            bytes_accessed=5 * TOK * FEATURES * 2,
            transcendentals=2 * HEADS * TOK * SPAN,
        ),
    )(
        *(
            pltpu.with_memory_space_constraint(array, pltpu.MemorySpace.HBM)
            for array in (
                section_input[0, 0],
                section_positions[0],
                saved_input[0, 0],
                saved_positions[0],
                cotangent[0, 0],
                norm_gains[:, 0],
                output_gains,
                plan[0],
            )
        )
    )
    produced, grads, totals = pl.pallas_call(
        place,
        out_shape=shapes,
        in_specs=[anywhere] * 3,
        out_specs=(anywhere,) * 3,
        scratch_shapes=[pltpu.SemaphoreType.DMA((3,))],
        compiler_params=pltpu.CompilerParams(vmem_limit_bytes=1024 * 1024),
    )(*results)
    return (produced[None, None], grads[None, None], totals.reshape(1, 3, FEATURES))


def solution(mesh):
    placed = (
        P("dp", "pipe", "ctx", None),
        P("dp", "pipe", "ctx"),
        P("dp", "pipe", "ctx", None),
        P("dp", "pipe", "ctx"),
        P("dp", "pipe", "ctx", None),
        P(None, "pipe", None, None),
        P(None, "pipe", None),
        P("dp", "pipe", None),
    )
    return jax.shard_map(
        functools.partial(local, {axis: mesh.shape[axis] for axis in ("dp", "pipe", "ctx")}),
        mesh=mesh,
        in_specs=placed,
        out_specs=(
            P("dp", "pipe", "ctx", None),
            P("dp", "pipe", "ctx", None),
            P("pipe", None, None),
        ),
        check_vma=False,
    )
```

```python
import functools

import jax
import jax.numpy as jnp
from jax import lax
from jax.experimental import pallas as pl
from jax.experimental.pallas import tpu as pltpu
from jax.sharding import PartitionSpec as P

HEADS = 16
HEAD_DIM = 128
FEATURES = 2048
WINDOW = 512
TOK = 128
PAIR = 2 * TOK
SPAN = WINDOW + PAIR
SLOTS = HEADS // 2
OWN_AHEAD = 8
AHEAD = 4
PASS = 2
DELAY = 5
GATHER = 6
GROUP = SLOTS // 2
EPSILON = 1e-06
SCALE = HEAD_DIM**-0.5
LOG2E = 1.4426950408889634
MESH = pl.DeviceIdType.MESH
F32 = jnp.float32
BF16 = jnp.bfloat16
FAR, NEAR, OWN = 0, PAIR, 2 * PAIR


def dot(left, right, left_dim, right_dim):
    return lax.dot_general(
        left, right, (((left_dim,), (right_dim,)), ((), ())), preferred_element_type=F32
    )


def kernel(
    sizes,
    sec_ref,
    sec_pos,
    sav_ref,
    sav_pos,
    cot_ref,
    norm_ref,
    outg_ref,
    plan_ref,
    next_ref,
    up_ref,
    total_ref,
    keys,
    cot,
    pos,
    norm_in,
    outg_in,
    plan_in,
    gains,
    masks,
    grads,
    own,
    from_near,
    from_far,
    produced,
    dx,
    sums,
    parts,
    columns,
    shares,
    load_sem,
    small_sem,
    pos_sem,
    swap_recv,
    cot_recv,
    pair_recv,
    relay_recv,
    near_recv,
    far_recv,
    out_recv,
    send_sem,
    gain_sem,
):
    n = sizes["ctx"]
    c = lax.axis_index("ctx")
    side = lax.rem(c, 2)
    partner = c + 1 - 2 * side
    pipe = lax.axis_index("pipe")
    after = lax.rem(pipe + 1, sizes["pipe"])
    before = lax.rem(pipe + sizes["pipe"] - 1, sizes["pipe"])
    up, down = c + 2 < n, c >= 2
    down2 = c >= 4
    level, levels = c // 2, n // 2
    direct = levels <= 4
    replica, replicas = lax.axis_index("dp"), sizes["dp"]
    per = SLOTS // replicas
    SWAP, COT, POS, PAIRS, RELAY, NEARG, FARG, OUT = range(8)

    def part(first, which):
        return pl.ds(pl.multiple_of(first + which * TOK, TOK), TOK)

    def lanes_of(h):
        return pl.ds(pl.multiple_of(h * HEAD_DIM, HEAD_DIM), HEAD_DIM)

    def remote(source, target, send, recv, device):
        return pltpu.make_async_remote_copy(
            src_ref=source,
            dst_ref=target,
            send_sem=send,
            recv_sem=recv,
            device_id=device,
            device_id_type=MESH,
        )

    def wait_bytes(ref, sem):
        pltpu.make_async_copy(ref, ref, sem).wait()

    def load(which, j):
        source = (sav_ref, sec_ref, cot_ref)[which]
        mine = part(0, side) if which == 2 else part(OWN, side)
        target = cot.at[j, mine] if which == 2 else keys.at[which, j, mine]
        return pltpu.make_async_copy(
            source.at[:, lanes_of(side * SLOTS + j)], target, load_sem.at[which]
        )

    def swap_copy(t, j):
        mine = part(OWN, side)
        return remote(
            (sav_ref, sec_ref)[t].at[:, lanes_of((1 - side) * SLOTS + j)],
            keys.at[t, j, mine],
            send_sem.at[SWAP],
            swap_recv.at[SLOTS if t else j],
            {"ctx": partner},
        )

    def cot_copy(j):
        return remote(
            cot_ref.at[:, lanes_of((1 - side) * SLOTS + j)],
            cot.at[j, part(0, side)],
            send_sem.at[COT],
            cot_recv.at[j // GROUP],
            {"ctx": partner},
        )

    def pos_copy(t):
        return remote(
            (sav_pos, sec_pos)[t],
            pos.at[t, side],
            send_sem.at[POS],
            pos_sem.at[1],
            {"ctx": partner},
        )

    def pair_copy(s, which):
        t, j = s // SLOTS, lax.rem(s, SLOTS)
        return remote(
            keys.at[t, j, part(OWN, which)],
            keys.at[t, j, part(NEAR, which)],
            send_sem.at[PAIRS],
            pair_recv.at[s],
            {"ctx": c + 2},
        )

    def relay_copy(s):
        t, j = s // SLOTS, lax.rem(s, SLOTS)
        return remote(
            keys.at[t, j, pl.ds(NEAR, PAIR)],
            keys.at[t, j, pl.ds(FAR, PAIR)],
            send_sem.at[RELAY],
            relay_recv.at[s],
            {"ctx": c + 2},
        )

    def near_copy(j):
        return remote(
            grads.at[j, pl.ds(NEAR, PAIR)],
            from_near.at[j],
            send_sem.at[NEARG],
            near_recv.at[j],
            {"ctx": c - 2},
        )

    def far_copy(j):
        return remote(
            grads.at[j, pl.ds(FAR, PAIR)],
            from_far.at[j],
            send_sem.at[FARG],
            far_recv.at[j],
            {"ctx": c - 2},
        )

    def out_copy(kind, j, which):
        device = {"pipe": (after, before)[kind]}
        if which == 1:
            device["ctx"] = partner
        rows = part(0, side if which == 0 else 1 - side)
        return remote(
            (produced, dx)[kind].at[j, rows],
            (next_ref, up_ref)[kind].at[:, lanes_of(side * SLOTS + j)],
            send_sem.at[OUT + kind],
            out_recv.at[kind],
            device,
        )

    def gain_copy(source, target, kind, device):
        return remote(source, target, gain_sem.at[kind], gain_sem.at[kind + 1], device)

    def start_sum():
        parts[replica] = sums[replica]
        for k in range(1, replicas):
            peer = lax.rem(replica + k, replicas)
            gain_copy(sums.at[peer], parts.at[replica], 0, {"dp": peer}).start()

    def column_copy():
        if direct:
            return gain_copy(columns.at[level], columns.at[level], 2, {"ctx": side})
        return gain_copy(columns.at[0], columns.at[1], 2, {"ctx": c - 2})

    def start_column():
        if replicas > 1:
            wait_bytes(parts.at[pl.ds(0, replicas - 1)], gain_sem.at[1])
        total = parts[0]
        for which in range(1, replicas):
            total = total + parts[which]
        columns[level if direct else 0] = total
        if direct:
            pl.when(level > 0)(lambda: column_copy().start())

    def spread(k):
        gain_copy(shares.at[side * replicas + replica], shares.at[side * replicas + replica], 4, {"ctx": c + 2 * k}).start()

    def top_column():
        wait_bytes(columns.at[pl.ds(0, levels - 1)], gain_sem.at[3])
        total = columns[0]
        for which in range(1, levels):
            total = total + columns[which]
        shares[side * replicas + replica] = total * (1.0 / TOK)
        for k in range(1, levels):
            spread(k)

    def chain_column():
        @pl.when(up)
        def _():
            wait_bytes(columns.at[0], gain_sem.at[3])
            columns[0] = columns[0] + columns[1]

        pl.when(down)(lambda: column_copy().start())

        @pl.when(level == 0)
        def _():
            shares[side * replicas + replica] = columns[0] * (1.0 / TOK)

    def start_share():
        pl.when(level > 0)(lambda: wait_bytes(columns.at[0], gain_sem.at[5]))
        if not direct:
            pl.when(up)(lambda: spread(1))
        for k in range(replicas):
            peer = lax.rem(replica + k, replicas)
            for which in ([partner] if k == 0 else [c, partner]):
                gain_copy(
                    shares.at[side * replicas + replica],
                    shares.at[side * replicas + replica],
                    6,
                    {"ctx": which, "dp": peer},
                ).start()

    def wait_shares(kind):
        wait_bytes(shares.at[pl.ds(0, 2 * replicas - 1)], gain_sem.at[kind])

    def finish_total():
        wait_shares(7)
        for which in range(2):
            for chunk in range(replicas):
                for m in range(3):
                    first = m * HEADS + which * SLOTS + chunk * per
                    total_ref[pl.ds(first, per), :] = shares[which * replicas + chunk, pl.ds(m * per, per), :]

    def each(action):
        @pl.loop(0, SLOTS)
        def _(j):
            action(j)

    barrier = pltpu.get_barrier_semaphore()

    def greet(device):
        pl.semaphore_signal(barrier, inc=1, device_id=device, device_id_type=MESH)

    greet({"ctx": partner})
    greet({"pipe": after})
    greet({"ctx": partner, "pipe": after})
    count = 3
    if sizes["pipe"] > 2:
        greet({"pipe": before})
        greet({"ctx": partner, "pipe": before})
        count += 2
    for condition, device in ((up, c + 2), (down, c - 2)):
        pl.when(condition)(lambda: greet({"ctx": device}))
        count = count + condition.astype(jnp.int32)
    for k in range(1, replicas):
        greet({"dp": lax.rem(replica + k, replicas)})
        count += 1

    each(lambda j: load(0, j).start())
    small = (
        (norm_ref, norm_in),
        (outg_ref, outg_in),
        (plan_ref, plan_in),
        (sav_pos, pos.at[0, side]),
        (sec_pos, pos.at[1, side]),
    )
    for i, (source, target) in enumerate(small):
        pltpu.make_async_copy(source, target, small_sem.at[i]).start()
    each(lambda j: load(2, j).start())
    each(lambda j: load(1, j).start())
    wait_bytes(keys.at[0, :, pl.ds(0, TOK)], load_sem.at[0])
    pl.semaphore_wait(barrier, count)

    def pass_pair(s, which):
        pl.when(up)(lambda: pair_copy(s, which).start())

    def relay(s):
        @pl.when(down)
        def _():
            wait_bytes(keys.at[0, 0, pl.ds(NEAR, PAIR)], pair_recv.at[s])
            pl.when(up)(lambda: relay_copy(s).start())

    def wait_swap(s):
        @pl.when(s < SLOTS)
        def _():
            wait_bytes(keys.at[0, 0, pl.ds(0, TOK)], swap_recv.at[jnp.minimum(s, SLOTS)])

        pl.when(s == SLOTS)(
            lambda: wait_bytes(keys.at[0, :, pl.ds(0, TOK)], swap_recv.at[SLOTS])
        )

    swap_copy(0, 0).start()
    pass_pair(0, side)
    pass_pair(1, side)
    for t in range(2):
        pos_copy(t).start()

    def first_swaps(j):
        pl.when(j > 0)(lambda: swap_copy(0, j).start())
        pl.when((j > 1) & (j < OWN_AHEAD))(lambda: pass_pair(j, side))
        cot_copy(j).start()

    each(first_swaps)
    each(lambda j: swap_copy(1, j).start())

    for i, (source, target) in enumerate(small):
        pltpu.make_async_copy(source, target, small_sem.at[i]).wait()
    for which in range(2):
        lap = plan_in[0, which]
        gains[pl.ds(3 * which, 2), :] = jnp.where(lap == 1, norm_in[1], norm_in[0])
        gains[pl.ds(3 * which + 2, 1), :] = jnp.where(lap == 1, outg_in[1], outg_in[0])
    for reach, first in ((2, NEAR), (4, FAR)):

        @pl.when(c < reach)
        def _():
            @pl.loop(0, SLOTS)
            def _(j):
                for t in range(2):
                    keys[t, j, pl.ds(first, PAIR)] = jnp.zeros((PAIR, HEAD_DIM), BF16)

    for s in range(AHEAD):
        wait_swap(s)
        pass_pair(s, 1 - side)

    wait_bytes(pos.at[:, 0], pos_sem.at[1])
    distance = (
        lax.broadcasted_iota(jnp.int32, (SPAN, TOK), 1)
        + WINDOW
        - lax.broadcasted_iota(jnp.int32, (SPAN, TOK), 0)
    )
    for t in range(2):
        for which in range(2):
            apart = distance + which * TOK
            allowed = (apart >= 0) & (apart < WINDOW) & (apart <= pos[t, which])
            masks[t, :, pl.ds(which * TOK, TOK)] = jnp.where(allowed, 1.0, 0.0).astype(F32)

    wait_bytes(cot.at[:, pl.ds(0, TOK)], load_sem.at[2])
    wait_bytes(keys.at[1, :, pl.ds(0, TOK)], load_sem.at[1])
    for s in range(PASS):
        relay(s)

    def normed(x):
        wide = x.astype(F32)
        inverse = lax.rsqrt(jnp.mean(wide * wide, axis=-1, keepdims=True) + EPSILON)
        return wide * inverse, inverse

    def weights(t, k, q, queries):
        w = jnp.exp2(dot(k, q, 1, 1) * (SCALE * LOG2E)) * masks[t, :, queries]
        return w, 1.0 / jnp.sum(w, axis=0, keepdims=True)

    def backward(j):
        wide = lanes_of(side * SLOTS + j)
        a, b, g = (gains[pl.ds(3 + m, 1), wide] for m in range(3))
        x = keys[0, j]
        n_all, inverse = normed(x)
        k = (n_all * b).astype(BF16)
        q = (n_all[WINDOW:] * a).astype(BF16)
        w, sum_inverse = weights(0, k, q, pl.ds(0, PAIR))
        prob = w * sum_inverse
        p = prob.astype(BF16)
        ct = cot[j].astype(F32)
        d_mix = (ct * g).astype(BF16)
        d_prob = dot(x, d_mix, 1, 1)
        delta = jnp.sum(prob * d_prob, axis=0, keepdims=True)
        d_score = (prob * (d_prob - delta)).astype(BF16)
        d_k = dot(d_score, q, 1, 0)
        d_q = dot(k, d_score, 0, 0).T
        mixed = dot(p, cot[j], 1, 0)
        d_value = mixed * g
        n_own = n_all[WINDOW:]
        d_n = d_k * (b * SCALE)
        d_n_own = d_n[WINDOW:] + d_q * (a * SCALE)

        def through_norm(d, value, scale):
            return scale * (d - value * jnp.mean(d * value, axis=-1, keepdims=True))

        grads[j] = (
            d_value[:WINDOW] + through_norm(d_n[:WINDOW], n_all[:WINDOW], inverse[:WINDOW])
        ).astype(BF16)
        own[j] = d_value[WINDOW:] + through_norm(d_n_own, n_own, inverse[WINDOW:]) + ct
        gained = (
            jnp.sum(d_q * n_own, axis=0, keepdims=True) * SCALE,
            jnp.sum(d_k * n_all, axis=0, keepdims=True) * SCALE,
            jnp.sum(mixed * x, axis=0, keepdims=True),
        )
        for m in range(3):
            sums[j // per, pl.ds(m * per + lax.rem(j, per), 1), :] = gained[m]

    def forward(j):
        wide = lanes_of(side * SLOTS + j)
        a, b, g = (gains[pl.ds(m, 1), wide] for m in range(3))

        def attend(first, length, queries):
            x = keys[1, j, pl.ds(first, length)]
            k = (normed(x)[0] * b).astype(BF16)
            found = []
            for q, rows in queries:
                scores = dot(k, q, 1, 1) * (SCALE * LOG2E)
                w = jnp.exp2(scores) * masks[1, pl.ds(first, length), part(0, rows)]
                found.append((jnp.sum(w, axis=0, keepdims=True), dot(x, w.astype(BF16), 0, 0)))
            return found

        queries = []
        for rows in (1 - side, side):
            mine = keys[1, j, part(OWN, rows)]
            queries.append(((normed(mine)[0] * a).astype(BF16), rows))
        close = attend(NEAR, SPAN - NEAR, queries)
        await_far(j + SLOTS)
        distant = attend(FAR, NEAR, queries)
        for which, (_, rows) in enumerate(queries):
            (sum_near, mix_near), (sum_far, mix_far) = close[which], distant[which]
            mix = ((mix_near + mix_far) * (1.0 / (sum_near + sum_far))).T
            mine = keys[1, j, part(OWN, rows)].astype(F32)
            produced[j, part(0, rows)] = (mine + g * mix).astype(BF16)
            out_copy(0, j, 1 - which).start()

    def feed(s, total):
        @pl.when(s + AHEAD < total)
        def _():
            wait_swap(s + AHEAD)
            pass_pair(s + AHEAD, 1 - side)

        pl.when(s + OWN_AHEAD < total)(lambda: pass_pair(s + OWN_AHEAD, side))

        pl.when(s + PASS < total)(lambda: relay(s + PASS))

    def await_far(s):
        pl.when(down2)(lambda: wait_bytes(keys.at[0, 0, pl.ds(FAR, PAIR)], relay_recv.at[s]))

    def send_near(j):
        @pl.when(up & down)
        def _():
            far_copy(j).wait_recv()
            near = grads[j, pl.ds(NEAR, PAIR)].astype(F32) + from_far[j].astype(F32)
            grads[j, pl.ds(NEAR, PAIR)] = near.astype(BF16)
            near_copy(j).start()

    def first(j):
        feed(j, 2 * SLOTS)
        await_far(j)
        pl.when(lax.rem(j, GROUP) == 0)(
            lambda: wait_bytes(cot.at[pl.ds(0, GROUP), pl.ds(0, TOK)], cot_recv.at[j // GROUP])
        )
        backward(j)
        pl.when(down2)(lambda: far_copy(j).start())
        pl.when(down & jnp.logical_not(up))(lambda: near_copy(j).start())
        pl.when(j >= DELAY)(lambda: send_near(jnp.maximum(j - DELAY, 0)))

    each(first)
    start_sum()

    def send_dx(j):
        @pl.when(up)
        def _():
            near_copy(j).wait_recv()
            own[j] = own[j] + from_near[j].astype(F32)

        dx[j] = own[j].astype(BF16)
        for which in range(2):
            out_copy(1, j, which).start()

    def last(j):
        feed(j + SLOTS, 2 * SLOTS)
        pl.when(j < DELAY)(lambda: send_near(jnp.minimum(j + SLOTS - DELAY, SLOTS - 1)))
        send_dx(j)
        pl.when(j == 1)(start_column)
        if direct:
            pl.when((j == 4) & (level == 0))(top_column)
            pl.when(j == 6)(start_share)
        forward(j)

    each(last)
    if not direct:
        chain_column()
        start_share()
    finish_total()

    swapped = keys.at[:, :, pl.ds(0, TOK)]
    paired = keys.at[:, :, pl.ds(0, PAIR)]
    wait_bytes(swapped, send_sem.at[SWAP])
    wait_bytes(cot.at[:, pl.ds(0, TOK)], send_sem.at[COT])
    wait_bytes(pos.at[:, 0], send_sem.at[POS])
    pl.when(up)(lambda: wait_bytes(paired, send_sem.at[PAIRS]))
    pl.when(up & down)(lambda: wait_bytes(paired, send_sem.at[RELAY]))
    pl.when(down)(lambda: wait_bytes(from_near, send_sem.at[NEARG]))
    pl.when(down2)(lambda: wait_bytes(from_far, send_sem.at[FARG]))
    if replicas > 1:
        wait_bytes(sums.at[pl.ds(0, replicas - 1)], gain_sem.at[0])
    pl.when(level > 0)(lambda: wait_bytes(columns.at[0], gain_sem.at[2]))
    if direct:
        pl.when(level == 0)(lambda: wait_bytes(columns.at[pl.ds(0, levels - 1)], gain_sem.at[4]))
    else:
        pl.when(up)(lambda: wait_bytes(columns.at[0], gain_sem.at[4]))
    wait_shares(6)
    for kind, (sent, target) in enumerate(((produced, next_ref), (dx, up_ref))):
        wait_bytes(sent, send_sem.at[OUT + kind])
        wait_bytes(target, out_recv.at[kind])


def place(produced_ref, grads_ref, total_ref, next_ref, up_ref, gain_ref, sem):
    pairs = ((produced_ref, next_ref), (grads_ref, up_ref), (total_ref, gain_ref))
    copies = [
        pltpu.make_async_copy(source, target, sem.at[i])
        for i, (source, target) in enumerate(pairs)
    ]
    for copy in copies:
        copy.start()
    for copy in copies:
        copy.wait()


def local(
    sizes,
    section_input,
    section_positions,
    saved_input,
    saved_positions,
    cotangent,
    norm_gains,
    output_gains,
    plan,
):
    replicas, levels = sizes["dp"], sizes["ctx"] // 2
    part_shape = (3 * SLOTS // replicas, HEAD_DIM)
    anywhere = pl.BlockSpec(memory_space=pl.ANY)
    in_vmem = pl.BlockSpec(memory_space=pltpu.VMEM)
    shapes = (
        jax.ShapeDtypeStruct((TOK, FEATURES), BF16),
        jax.ShapeDtypeStruct((TOK, FEATURES), BF16),
        jax.ShapeDtypeStruct((3 * HEADS, HEAD_DIM), F32),
    )
    results = pl.pallas_call(
        functools.partial(kernel, sizes),
        out_shape=shapes,
        in_specs=[anywhere] * 8,
        out_specs=(anywhere, anywhere, in_vmem),
        scratch_shapes=[
            pltpu.VMEM((2, SLOTS, SPAN, HEAD_DIM), BF16),
            pltpu.VMEM((SLOTS, PAIR, HEAD_DIM), BF16),
            pltpu.VMEM((2, 2, 1, TOK), jnp.int32),
            pltpu.VMEM((2, 2, FEATURES), F32),
            pltpu.VMEM((2, 1, FEATURES), F32),
            pltpu.SMEM((1, 2), jnp.int32),
            pltpu.VMEM((8, FEATURES), F32),
            pltpu.VMEM((2, SPAN, PAIR), F32),
            pltpu.VMEM((SLOTS, WINDOW, HEAD_DIM), BF16),
            pltpu.VMEM((SLOTS, PAIR, HEAD_DIM), F32),
            pltpu.VMEM((SLOTS, PAIR, HEAD_DIM), BF16),
            pltpu.VMEM((SLOTS, PAIR, HEAD_DIM), BF16),
            pltpu.VMEM((SLOTS, PAIR, HEAD_DIM), BF16),
            pltpu.VMEM((SLOTS, PAIR, HEAD_DIM), BF16),
            pltpu.VMEM((replicas, *part_shape), F32),
            pltpu.VMEM((replicas, *part_shape), F32),
            pltpu.VMEM((levels, *part_shape), F32),
            pltpu.VMEM((2 * replicas, *part_shape), F32),
            pltpu.SemaphoreType.DMA((3,)),
            pltpu.SemaphoreType.DMA((5,)),
            pltpu.SemaphoreType.DMA((2,)),
            pltpu.SemaphoreType.DMA((SLOTS + 1,)),
            pltpu.SemaphoreType.DMA((2,)),
            pltpu.SemaphoreType.DMA((2 * SLOTS,)),
            pltpu.SemaphoreType.DMA((2 * SLOTS,)),
            pltpu.SemaphoreType.DMA((SLOTS,)),
            pltpu.SemaphoreType.DMA((SLOTS,)),
            pltpu.SemaphoreType.DMA((2,)),
            pltpu.SemaphoreType.DMA((9,)),
            pltpu.SemaphoreType.DMA((8,)),
        ],
        compiler_params=pltpu.CompilerParams(
            collective_id=0, has_side_effects=True, vmem_limit_bytes=24 * 1024 * 1024
        ),
        cost_estimate=pl.CostEstimate(
            flops=9 * 2 * TOK * SPAN * FEATURES,
            bytes_accessed=5 * TOK * FEATURES * 2,
            transcendentals=2 * HEADS * TOK * SPAN,
        ),
    )(
        *(
            pltpu.with_memory_space_constraint(array, pltpu.MemorySpace.HBM)
            for array in (
                section_input[0, 0],
                section_positions[0],
                saved_input[0, 0],
                saved_positions[0],
                cotangent[0, 0],
                norm_gains[:, 0],
                output_gains,
                plan[0],
            )
        )
    )
    produced, grads, totals = pl.pallas_call(
        place,
        out_shape=shapes,
        in_specs=[anywhere] * 3,
        out_specs=(anywhere,) * 3,
        scratch_shapes=[pltpu.SemaphoreType.DMA((3,))],
        compiler_params=pltpu.CompilerParams(vmem_limit_bytes=1024 * 1024),
    )(*results)
    return (produced[None, None], grads[None, None], totals.reshape(1, 3, FEATURES))


def solution(mesh):
    placed = (
        P("dp", "pipe", "ctx", None),
        P("dp", "pipe", "ctx"),
        P("dp", "pipe", "ctx", None),
        P("dp", "pipe", "ctx"),
        P("dp", "pipe", "ctx", None),
        P(None, "pipe", None, None),
        P(None, "pipe", None),
        P("dp", "pipe", None),
    )
    return jax.shard_map(
        functools.partial(local, {axis: mesh.shape[axis] for axis in ("dp", "pipe", "ctx")}),
        mesh=mesh,
        in_specs=placed,
        out_specs=(
            P("dp", "pipe", "ctx", None),
            P("dp", "pipe", "ctx", None),
            P("pipe", None, None),
        ),
        check_vma=False,
    )
```

```python
import functools

import jax
import jax.numpy as jnp
from jax import lax
from jax.experimental import pallas as pl
from jax.experimental.pallas import tpu as pltpu
from jax.sharding import PartitionSpec as P

HEADS = 16
HEAD_DIM = 128
FEATURES = 2048
WINDOW = 512
TOK = 128
PAIR = 2 * TOK
SPAN = WINDOW + PAIR
SLOTS = HEADS // 2
OWN_AHEAD = 8
AHEAD = 4
PASS = 2
DELAY = 5
GATHER = 6
GROUP = SLOTS // 2
EPSILON = 1e-06
SCALE = HEAD_DIM**-0.5
LOG2E = 1.4426950408889634
MESH = pl.DeviceIdType.MESH
F32 = jnp.float32
BF16 = jnp.bfloat16
FAR, NEAR, OWN = 0, PAIR, 2 * PAIR


def dot(left, right, left_dim, right_dim):
    return lax.dot_general(
        left, right, (((left_dim,), (right_dim,)), ((), ())), preferred_element_type=F32
    )


def kernel(
    sizes,
    sec_ref,
    sec_pos,
    sav_ref,
    sav_pos,
    cot_ref,
    norm_ref,
    outg_ref,
    plan_ref,
    next_ref,
    up_ref,
    total_ref,
    keys,
    cot,
    pos,
    norm_in,
    outg_in,
    plan_in,
    gains,
    masks,
    grads,
    own,
    from_near,
    from_far,
    produced,
    dx,
    sums,
    parts,
    columns,
    shares,
    load_sem,
    small_sem,
    pos_sem,
    swap_recv,
    cot_recv,
    pair_recv,
    relay_recv,
    near_recv,
    far_recv,
    out_recv,
    send_sem,
    gain_sem,
):
    n = sizes["ctx"]
    c = lax.axis_index("ctx")
    side = lax.rem(c, 2)
    partner = c + 1 - 2 * side
    pipe = lax.axis_index("pipe")
    after = lax.rem(pipe + 1, sizes["pipe"])
    before = lax.rem(pipe + sizes["pipe"] - 1, sizes["pipe"])
    up, down = c + 2 < n, c >= 2
    down2 = c >= 4
    level, levels = c // 2, n // 2
    direct = levels <= 4
    replica, replicas = lax.axis_index("dp"), sizes["dp"]
    per = SLOTS // replicas
    SWAP, COT, POS, PAIRS, RELAY, NEARG, FARG, OUT = range(8)

    def part(first, which):
        return pl.ds(pl.multiple_of(first + which * TOK, TOK), TOK)

    def lanes_of(h):
        return pl.ds(pl.multiple_of(h * HEAD_DIM, HEAD_DIM), HEAD_DIM)

    def remote(source, target, send, recv, device):
        return pltpu.make_async_remote_copy(
            src_ref=source,
            dst_ref=target,
            send_sem=send,
            recv_sem=recv,
            device_id=device,
            device_id_type=MESH,
        )

    def wait_bytes(ref, sem):
        pltpu.make_async_copy(ref, ref, sem).wait()

    def load(which, j):
        source = (sav_ref, sec_ref, cot_ref)[which]
        mine = part(0, side) if which == 2 else part(OWN, side)
        target = cot.at[j, mine] if which == 2 else keys.at[which, j, mine]
        return pltpu.make_async_copy(
            source.at[:, lanes_of(side * SLOTS + j)], target, load_sem.at[which]
        )

    def swap_copy(t, j):
        mine = part(OWN, side)
        return remote(
            (sav_ref, sec_ref)[t].at[:, lanes_of((1 - side) * SLOTS + j)],
            keys.at[t, j, mine],
            send_sem.at[SWAP],
            swap_recv.at[SLOTS if t else j],
            {"ctx": partner},
        )

    def cot_copy(j):
        return remote(
            cot_ref.at[:, lanes_of((1 - side) * SLOTS + j)],
            cot.at[j, part(0, side)],
            send_sem.at[COT],
            cot_recv.at[j // GROUP],
            {"ctx": partner},
        )

    def pos_copy(t):
        return remote(
            (sav_pos, sec_pos)[t],
            pos.at[t, side],
            send_sem.at[POS],
            pos_sem.at[1],
            {"ctx": partner},
        )

    def pair_copy(s, which):
        t, j = s // SLOTS, lax.rem(s, SLOTS)
        return remote(
            keys.at[t, j, part(OWN, which)],
            keys.at[t, j, part(NEAR, which)],
            send_sem.at[PAIRS],
            pair_recv.at[s],
            {"ctx": c + 2},
        )

    def relay_copy(s):
        t, j = s // SLOTS, lax.rem(s, SLOTS)
        return remote(
            keys.at[t, j, pl.ds(NEAR, PAIR)],
            keys.at[t, j, pl.ds(FAR, PAIR)],
            send_sem.at[RELAY],
            relay_recv.at[s],
            {"ctx": c + 2},
        )

    def near_copy(j):
        return remote(
            grads.at[j, pl.ds(NEAR, PAIR)],
            from_near.at[j],
            send_sem.at[NEARG],
            near_recv.at[j // 2],
            {"ctx": c - 2},
        )

    def far_copy(j):
        return remote(
            grads.at[j, pl.ds(FAR, PAIR)],
            from_far.at[j],
            send_sem.at[FARG],
            far_recv.at[j],
            {"ctx": c - 2},
        )

    def out_copy(kind, j, which):
        device = {"pipe": (after, before)[kind]}
        if which == 1:
            device["ctx"] = partner
        rows = part(0, side if which == 0 else 1 - side)
        return remote(
            (produced, dx)[kind].at[j, rows],
            (next_ref, up_ref)[kind].at[:, lanes_of(side * SLOTS + j)],
            send_sem.at[OUT + kind],
            out_recv.at[kind],
            device,
        )

    def gain_copy(source, target, kind, device):
        return remote(source, target, gain_sem.at[kind], gain_sem.at[kind + 1], device)

    def start_sum():
        parts[replica] = sums[replica]
        for k in range(1, replicas):
            peer = lax.rem(replica + k, replicas)
            gain_copy(sums.at[peer], parts.at[replica], 0, {"dp": peer}).start()

    def column_copy():
        if direct:
            return gain_copy(columns.at[level], columns.at[level], 2, {"ctx": side})
        return gain_copy(columns.at[0], columns.at[1], 2, {"ctx": c - 2})

    def start_column():
        if replicas > 1:
            wait_bytes(parts.at[pl.ds(0, replicas - 1)], gain_sem.at[1])
        total = parts[0]
        for which in range(1, replicas):
            total = total + parts[which]
        columns[level if direct else 0] = total
        if direct:
            pl.when(level > 0)(lambda: column_copy().start())

    def spread(k):
        gain_copy(shares.at[side * replicas + replica], shares.at[side * replicas + replica], 4, {"ctx": c + 2 * k}).start()

    def top_column():
        wait_bytes(columns.at[pl.ds(0, levels - 1)], gain_sem.at[3])
        total = columns[0]
        for which in range(1, levels):
            total = total + columns[which]
        shares[side * replicas + replica] = total * (1.0 / TOK)
        for k in range(1, levels):
            spread(k)

    def chain_column():
        @pl.when(up)
        def _():
            wait_bytes(columns.at[0], gain_sem.at[3])
            columns[0] = columns[0] + columns[1]

        pl.when(down)(lambda: column_copy().start())

        @pl.when(level == 0)
        def _():
            shares[side * replicas + replica] = columns[0] * (1.0 / TOK)

    def start_share():
        pl.when(level > 0)(lambda: wait_bytes(columns.at[0], gain_sem.at[5]))
        if not direct:
            pl.when(up)(lambda: spread(1))
        for k in range(replicas):
            peer = lax.rem(replica + k, replicas)
            for which in ([partner] if k == 0 else [c, partner]):
                gain_copy(
                    shares.at[side * replicas + replica],
                    shares.at[side * replicas + replica],
                    6,
                    {"ctx": which, "dp": peer},
                ).start()

    def wait_shares(kind):
        wait_bytes(shares.at[pl.ds(0, 2 * replicas - 1)], gain_sem.at[kind])

    def finish_total():
        wait_shares(7)
        for which in range(2):
            for chunk in range(replicas):
                for m in range(3):
                    first = m * HEADS + which * SLOTS + chunk * per
                    total_ref[pl.ds(first, per), :] = shares[which * replicas + chunk, pl.ds(m * per, per), :]

    def each(action):
        @pl.loop(0, SLOTS)
        def _(j):
            action(j)

    barrier = pltpu.get_barrier_semaphore()

    def greet(device):
        pl.semaphore_signal(barrier, inc=1, device_id=device, device_id_type=MESH)

    greet({"ctx": partner})
    greet({"pipe": after})
    greet({"ctx": partner, "pipe": after})
    count = 3
    if sizes["pipe"] > 2:
        greet({"pipe": before})
        greet({"ctx": partner, "pipe": before})
        count += 2
    for condition, device in ((up, c + 2), (down, c - 2)):
        pl.when(condition)(lambda: greet({"ctx": device}))
        count = count + condition.astype(jnp.int32)
    for k in range(1, replicas):
        greet({"dp": lax.rem(replica + k, replicas)})
        count += 1

    each(lambda j: load(0, j).start())
    small = (
        (norm_ref, norm_in),
        (outg_ref, outg_in),
        (plan_ref, plan_in),
        (sav_pos, pos.at[0, side]),
        (sec_pos, pos.at[1, side]),
    )
    for i, (source, target) in enumerate(small):
        pltpu.make_async_copy(source, target, small_sem.at[i]).start()
    each(lambda j: load(2, j).start())
    each(lambda j: load(1, j).start())
    wait_bytes(keys.at[0, :, pl.ds(0, TOK)], load_sem.at[0])
    pl.semaphore_wait(barrier, count)

    def pass_pair(s, which):
        pl.when(up)(lambda: pair_copy(s, which).start())

    def relay(s):
        @pl.when(down)
        def _():
            wait_bytes(keys.at[0, 0, pl.ds(NEAR, PAIR)], pair_recv.at[s])
            pl.when(up)(lambda: relay_copy(s).start())

    def wait_swap(s):
        @pl.when(s < SLOTS)
        def _():
            wait_bytes(keys.at[0, 0, pl.ds(0, TOK)], swap_recv.at[jnp.minimum(s, SLOTS)])

        pl.when(s == SLOTS)(
            lambda: wait_bytes(keys.at[0, :, pl.ds(0, TOK)], swap_recv.at[SLOTS])
        )

    swap_copy(0, 0).start()
    pass_pair(0, side)
    pass_pair(1, side)
    for t in range(2):
        pos_copy(t).start()

    def first_swaps(j):
        pl.when(j > 0)(lambda: swap_copy(0, j).start())
        pl.when((j > 1) & (j < OWN_AHEAD))(lambda: pass_pair(j, side))
        cot_copy(j).start()

    each(first_swaps)
    each(lambda j: swap_copy(1, j).start())

    for i, (source, target) in enumerate(small):
        pltpu.make_async_copy(source, target, small_sem.at[i]).wait()
    for which in range(2):
        lap = plan_in[0, which]
        gains[pl.ds(3 * which, 2), :] = jnp.where(lap == 1, norm_in[1], norm_in[0])
        gains[pl.ds(3 * which + 2, 1), :] = jnp.where(lap == 1, outg_in[1], outg_in[0])
    for reach, first in ((2, NEAR), (4, FAR)):

        @pl.when(c < reach)
        def _():
            @pl.loop(0, SLOTS)
            def _(j):
                for t in range(2):
                    keys[t, j, pl.ds(first, PAIR)] = jnp.zeros((PAIR, HEAD_DIM), BF16)

    for s in range(AHEAD):
        wait_swap(s)
        pass_pair(s, 1 - side)

    wait_bytes(pos.at[:, 0], pos_sem.at[1])
    distance = (
        lax.broadcasted_iota(jnp.int32, (SPAN, TOK), 1)
        + WINDOW
        - lax.broadcasted_iota(jnp.int32, (SPAN, TOK), 0)
    )
    for t in range(2):
        for which in range(2):
            apart = distance + which * TOK
            allowed = (apart >= 0) & (apart < WINDOW) & (apart <= pos[t, which])
            masks[t, :, pl.ds(which * TOK, TOK)] = jnp.where(allowed, 1.0, 0.0).astype(F32)

    wait_bytes(cot.at[:, pl.ds(0, TOK)], load_sem.at[2])
    wait_bytes(keys.at[1, :, pl.ds(0, TOK)], load_sem.at[1])
    for s in range(PASS):
        relay(s)

    def normed(x):
        wide = x.astype(F32)
        inverse = lax.rsqrt(jnp.mean(wide * wide, axis=-1, keepdims=True) + EPSILON)
        return wide * inverse, inverse

    def weights(t, k, q, queries):
        w = jnp.exp2(dot(k, q, 1, 1) * (SCALE * LOG2E)) * masks[t, :, queries]
        return w, 1.0 / jnp.sum(w, axis=0, keepdims=True)

    def backward(j):
        wide = lanes_of(side * SLOTS + j)
        a, b, g = (gains[pl.ds(3 + m, 1), wide] for m in range(3))
        x = keys[0, j]
        n_all, inverse = normed(x)
        k = (n_all * b).astype(BF16)
        q = (n_all[WINDOW:] * a).astype(BF16)
        w, sum_inverse = weights(0, k, q, pl.ds(0, PAIR))
        prob = w * sum_inverse
        p = prob.astype(BF16)
        ct = cot[j].astype(F32)
        d_mix = (ct * g).astype(BF16)
        d_prob = dot(x, d_mix, 1, 1)
        delta = jnp.sum(prob * d_prob, axis=0, keepdims=True)
        d_score = (prob * (d_prob - delta)).astype(BF16)
        d_k = dot(d_score, q, 1, 0)
        d_q = dot(k, d_score, 0, 0).T
        mixed = dot(p, cot[j], 1, 0)
        d_value = mixed * g
        n_own = n_all[WINDOW:]
        d_n = d_k * (b * SCALE)
        d_n_own = d_n[WINDOW:] + d_q * (a * SCALE)

        def through_norm(d, value, scale):
            return scale * (d - value * jnp.mean(d * value, axis=-1, keepdims=True))

        grads[j] = (
            d_value[:WINDOW] + through_norm(d_n[:WINDOW], n_all[:WINDOW], inverse[:WINDOW])
        ).astype(BF16)
        own[j] = d_value[WINDOW:] + through_norm(d_n_own, n_own, inverse[WINDOW:]) + ct
        gained = (
            jnp.sum(d_q * n_own, axis=0, keepdims=True) * SCALE,
            jnp.sum(d_k * n_all, axis=0, keepdims=True) * SCALE,
            jnp.sum(mixed * x, axis=0, keepdims=True),
        )
        for m in range(3):
            sums[j // per, pl.ds(m * per + lax.rem(j, per), 1), :] = gained[m]

    def forward(j):
        wide = lanes_of(side * SLOTS + j)
        a, b, g = (gains[pl.ds(m, 1), wide] for m in range(3))

        def attend(first, length, queries):
            x = keys[1, j, pl.ds(first, length)]
            k = (normed(x)[0] * b).astype(BF16)
            found = []
            for q, rows in queries:
                scores = dot(k, q, 1, 1) * (SCALE * LOG2E)
                w = jnp.exp2(scores) * masks[1, pl.ds(first, length), part(0, rows)]
                found.append((jnp.sum(w, axis=0, keepdims=True), dot(x, w.astype(BF16), 0, 0)))
            return found

        queries = []
        for rows in (1 - side, side):
            mine = keys[1, j, part(OWN, rows)]
            queries.append(((normed(mine)[0] * a).astype(BF16), rows))
        close = attend(NEAR, SPAN - NEAR, queries)
        await_far(j + SLOTS)
        distant = attend(FAR, NEAR, queries)
        for which, (_, rows) in enumerate(queries):
            (sum_near, mix_near), (sum_far, mix_far) = close[which], distant[which]
            mix = ((mix_near + mix_far) * (1.0 / (sum_near + sum_far))).T
            mine = keys[1, j, part(OWN, rows)].astype(F32)
            produced[j, part(0, rows)] = (mine + g * mix).astype(BF16)
            out_copy(0, j, 1 - which).start()

    def feed(s, total):
        @pl.when(s + AHEAD < total)
        def _():
            wait_swap(s + AHEAD)
            pass_pair(s + AHEAD, 1 - side)

        pl.when(s + OWN_AHEAD < total)(lambda: pass_pair(s + OWN_AHEAD, side))

        pl.when(s + PASS < total)(lambda: relay(s + PASS))

    def await_far(s):
        pl.when(down2)(lambda: wait_bytes(keys.at[0, 0, pl.ds(FAR, PAIR)], relay_recv.at[s]))

    def send_near(j):
        @pl.when(up & down)
        def _():
            far_copy(j).wait_recv()
            near = grads[j, pl.ds(NEAR, PAIR)].astype(F32) + from_far[j].astype(F32)
            grads[j, pl.ds(NEAR, PAIR)] = near.astype(BF16)
            near_copy(j).start()

    def first(j):
        feed(j, 2 * SLOTS)
        await_far(j)
        pl.when(lax.rem(j, GROUP) == 0)(
            lambda: wait_bytes(cot.at[pl.ds(0, GROUP), pl.ds(0, TOK)], cot_recv.at[j // GROUP])
        )
        backward(j)
        pl.when(down2)(lambda: far_copy(j).start())
        pl.when(down & jnp.logical_not(up))(lambda: near_copy(j).start())
        pl.when(j >= DELAY)(lambda: send_near(jnp.maximum(j - DELAY, 0)))

    each(first)
    start_sum()

    def send_dx(j):
        @pl.when(up)
        def _():
            pl.when(lax.rem(j, 2) == 0)(
                lambda: wait_bytes(from_near.at[pl.ds(0, 2)], near_recv.at[j // 2])
            )
            own[j] = own[j] + from_near[j].astype(F32)

        dx[j] = own[j].astype(BF16)
        for which in range(2):
            out_copy(1, j, which).start()

    def last(j):
        feed(j + SLOTS, 2 * SLOTS)
        pl.when(j < DELAY)(lambda: send_near(jnp.minimum(j + SLOTS - DELAY, SLOTS - 1)))
        send_dx(j)
        pl.when(j == 1)(start_column)
        if direct:
            pl.when((j == 4) & (level == 0))(top_column)
            pl.when(j == 6)(start_share)
        forward(j)

    each(last)
    if not direct:
        chain_column()
        start_share()
    finish_total()

    swapped = keys.at[:, :, pl.ds(0, TOK)]
    paired = keys.at[:, :, pl.ds(0, PAIR)]
    wait_bytes(swapped, send_sem.at[SWAP])
    wait_bytes(cot.at[:, pl.ds(0, TOK)], send_sem.at[COT])
    wait_bytes(pos.at[:, 0], send_sem.at[POS])
    pl.when(up)(lambda: wait_bytes(paired, send_sem.at[PAIRS]))
    pl.when(up & down)(lambda: wait_bytes(paired, send_sem.at[RELAY]))
    pl.when(down)(lambda: wait_bytes(from_near, send_sem.at[NEARG]))
    pl.when(down2)(lambda: wait_bytes(from_far, send_sem.at[FARG]))
    if replicas > 1:
        wait_bytes(sums.at[pl.ds(0, replicas - 1)], gain_sem.at[0])
    pl.when(level > 0)(lambda: wait_bytes(columns.at[0], gain_sem.at[2]))
    if direct:
        pl.when(level == 0)(lambda: wait_bytes(columns.at[pl.ds(0, levels - 1)], gain_sem.at[4]))
    else:
        pl.when(up)(lambda: wait_bytes(columns.at[0], gain_sem.at[4]))
    wait_shares(6)
    for kind, (sent, target) in enumerate(((produced, next_ref), (dx, up_ref))):
        wait_bytes(sent, send_sem.at[OUT + kind])
        wait_bytes(target, out_recv.at[kind])


def place(produced_ref, grads_ref, total_ref, next_ref, up_ref, gain_ref, sem):
    pairs = ((produced_ref, next_ref), (grads_ref, up_ref), (total_ref, gain_ref))
    copies = [
        pltpu.make_async_copy(source, target, sem.at[i])
        for i, (source, target) in enumerate(pairs)
    ]
    for copy in copies:
        copy.start()
    for copy in copies:
        copy.wait()


def local(
    sizes,
    section_input,
    section_positions,
    saved_input,
    saved_positions,
    cotangent,
    norm_gains,
    output_gains,
    plan,
):
    replicas, levels = sizes["dp"], sizes["ctx"] // 2
    part_shape = (3 * SLOTS // replicas, HEAD_DIM)
    anywhere = pl.BlockSpec(memory_space=pl.ANY)
    in_vmem = pl.BlockSpec(memory_space=pltpu.VMEM)
    shapes = (
        jax.ShapeDtypeStruct((TOK, FEATURES), BF16),
        jax.ShapeDtypeStruct((TOK, FEATURES), BF16),
        jax.ShapeDtypeStruct((3 * HEADS, HEAD_DIM), F32),
    )
    results = pl.pallas_call(
        functools.partial(kernel, sizes),
        out_shape=shapes,
        in_specs=[anywhere] * 8,
        out_specs=(anywhere, anywhere, in_vmem),
        scratch_shapes=[
            pltpu.VMEM((2, SLOTS, SPAN, HEAD_DIM), BF16),
            pltpu.VMEM((SLOTS, PAIR, HEAD_DIM), BF16),
            pltpu.VMEM((2, 2, 1, TOK), jnp.int32),
            pltpu.VMEM((2, 2, FEATURES), F32),
            pltpu.VMEM((2, 1, FEATURES), F32),
            pltpu.SMEM((1, 2), jnp.int32),
            pltpu.VMEM((8, FEATURES), F32),
            pltpu.VMEM((2, SPAN, PAIR), F32),
            pltpu.VMEM((SLOTS, WINDOW, HEAD_DIM), BF16),
            pltpu.VMEM((SLOTS, PAIR, HEAD_DIM), F32),
            pltpu.VMEM((SLOTS, PAIR, HEAD_DIM), BF16),
            pltpu.VMEM((SLOTS, PAIR, HEAD_DIM), BF16),
            pltpu.VMEM((SLOTS, PAIR, HEAD_DIM), BF16),
            pltpu.VMEM((SLOTS, PAIR, HEAD_DIM), BF16),
            pltpu.VMEM((replicas, *part_shape), F32),
            pltpu.VMEM((replicas, *part_shape), F32),
            pltpu.VMEM((levels, *part_shape), F32),
            pltpu.VMEM((2 * replicas, *part_shape), F32),
            pltpu.SemaphoreType.DMA((3,)),
            pltpu.SemaphoreType.DMA((5,)),
            pltpu.SemaphoreType.DMA((2,)),
            pltpu.SemaphoreType.DMA((SLOTS + 1,)),
            pltpu.SemaphoreType.DMA((2,)),
            pltpu.SemaphoreType.DMA((2 * SLOTS,)),
            pltpu.SemaphoreType.DMA((2 * SLOTS,)),
            pltpu.SemaphoreType.DMA((SLOTS // 2,)),
            pltpu.SemaphoreType.DMA((SLOTS,)),
            pltpu.SemaphoreType.DMA((2,)),
            pltpu.SemaphoreType.DMA((9,)),
            pltpu.SemaphoreType.DMA((8,)),
        ],
        compiler_params=pltpu.CompilerParams(
            collective_id=0, has_side_effects=True, vmem_limit_bytes=24 * 1024 * 1024
        ),
        cost_estimate=pl.CostEstimate(
            flops=9 * 2 * TOK * SPAN * FEATURES,
            bytes_accessed=5 * TOK * FEATURES * 2,
            transcendentals=2 * HEADS * TOK * SPAN,
        ),
    )(
        *(
            pltpu.with_memory_space_constraint(array, pltpu.MemorySpace.HBM)
            for array in (
                section_input[0, 0],
                section_positions[0],
                saved_input[0, 0],
                saved_positions[0],
                cotangent[0, 0],
                norm_gains[:, 0],
                output_gains,
                plan[0],
            )
        )
    )
    produced, grads, totals = pl.pallas_call(
        place,
        out_shape=shapes,
        in_specs=[anywhere] * 3,
        out_specs=(anywhere,) * 3,
        scratch_shapes=[pltpu.SemaphoreType.DMA((3,))],
        compiler_params=pltpu.CompilerParams(vmem_limit_bytes=1024 * 1024),
    )(*results)
    return (produced[None, None], grads[None, None], totals.reshape(1, 3, FEATURES))


def solution(mesh):
    placed = (
        P("dp", "pipe", "ctx", None),
        P("dp", "pipe", "ctx"),
        P("dp", "pipe", "ctx", None),
        P("dp", "pipe", "ctx"),
        P("dp", "pipe", "ctx", None),
        P(None, "pipe", None, None),
        P(None, "pipe", None),
        P("dp", "pipe", None),
    )
    return jax.shard_map(
        functools.partial(local, {axis: mesh.shape[axis] for axis in ("dp", "pipe", "ctx")}),
        mesh=mesh,
        in_specs=placed,
        out_specs=(
            P("dp", "pipe", "ctx", None),
            P("dp", "pipe", "ctx", None),
            P("pipe", None, None),
        ),
        check_vma=False,
    )
```
